256 devices in a mesh: dp: 64 (over z, y, x_hi), fsdp: 4 (over x_lo, core).
Axes of the slice: x: 4 (x_hi: 2, x_lo: 2; x = x_hi * 2 + x_lo), y: 4, z: 8, core: 2. Of those that a mesh axis runs over, the one named last changes fastest.
Arguments:
- image_features: float32 [8192, 1152], P(('dp', 'fsdp')), may hold values from -1.5 to 1.5
- text_features: float32 [8192, 1152], P(('dp', 'fsdp')), may hold values from -1.5 to 1.5
- image_proj: float32 [1152, 1152], P(None, 'fsdp'), may hold values from -0.1875 to 0.1875
- text_proj: float32 [1152, 1152], P(None, 'fsdp'), may hold values from -0.1875 to 0.1875
Outputs:
- grad_image_features: float32 [8192, 1152], P(('dp', 'fsdp'))
- grad_text_features: float32 [8192, 1152], P(('dp', 'fsdp'))
- grad_image_proj: float32 [1152, 1152], P(None, 'fsdp')
- grad_text_proj: float32 [1152, 1152], P(None, 'fsdp')
The draws below stay inside these ranges and needn't reach their ends.
All inputs are finite; a program needn't handle non-finite values.
Results may differ from the reference program's by a relative error of at most 0.0003.
Values sent between devices are 32-bit elements; how exact they have to be, the bound alone decides.
A program may use at most 64 MiB of HBM per device.

```python
import jax
import jax.numpy as jnp
from jax import lax

D = 1152
E = 1152
SPAN = 128
BATCH = 8192


def block_scale(key, extent, shards, smallest, largest):
    level = 1.0
    for position, shards_of in shards:
        heights = jax.random.uniform(jax.random.fold_in(jax.random.fold_in(key, 6), position), (shards_of,), jnp.float32, smallest / len(shards), largest / len(shards))
        level = level * jnp.repeat(jnp.exp(heights), extent[position] // shards_of).reshape((-1,) + (1,) * (len(extent) - 1 - position))
    return level


def noise(own_key, extent, scale, bound, split=(), kind=jnp.bfloat16):
    result = scale * jax.random.normal(own_key, extent, jnp.float32)
    if split:
        result = result * block_scale(own_key, extent, split, -0.22, 0.18)
    return jnp.clip(result, -bound, bound).astype(kind)


def setup_inputs(seed: int = 0) -> dict:
    key_list = jax.random.split(jax.random.key(seed), 5)
    return {
        "image_features": noise(key_list[0], (BATCH, D), 0.25, 1.5, ((0, 256),), jnp.float32),
        "text_features": noise(key_list[1], (BATCH, D), 0.25, 1.5, ((0, 256),), jnp.float32),
        "image_proj": noise(key_list[2], (D, E), D ** -0.5, 0.1875, ((1, 4),), jnp.float32),
        "text_proj": noise(key_list[3], (D, E), D ** -0.5, 0.1875, ((1, 4),), jnp.float32),
    }


logit_scale = 100.0
logit_bias = -10.0
epsilon_norm = 1e-06

def normalize(values):
    inverse = lax.rsqrt(lax.optimization_barrier(jnp.sum(values * values, axis=1, keepdims=True)) + epsilon_norm)
    return (values * inverse, inverse)

def reference(image_features, text_features, image_proj, text_proj):
    highest = lax.Precision.HIGHEST
    image_raw = jnp.dot(image_features, image_proj, precision=highest, preferred_element_type=jnp.float32)
    text_raw = jnp.dot(text_features, text_proj, precision=highest, preferred_element_type=jnp.float32)
    image_unit, image_inverse = normalize(image_raw)
    text_unit, text_inverse = normalize(text_raw)
    block_count = BATCH // SPAN
    blocks = image_unit.reshape(block_count, SPAN, E)
    starts = jnp.arange(block_count, dtype=jnp.int32) * SPAN
    columns = lax.broadcasted_iota(jnp.int32, (SPAN, BATCH), 1)
    row_ids = lax.broadcasted_iota(jnp.int32, (SPAN, BATCH), 0)

    def block_step(text_sums, inputs):
        unit_block, first_row = inputs
        logits = logit_scale * jnp.dot(unit_block, text_unit.T, precision=highest, preferred_element_type=jnp.float32) + logit_bias
        labels = (row_ids + first_row == columns).astype(logits.dtype)
        pair_grad = jax.nn.sigmoid(logits) - labels
        image_part = logit_scale * jnp.dot(pair_grad, text_unit, precision=highest, preferred_element_type=jnp.float32)
        text_sums = text_sums + logit_scale * jnp.dot(pair_grad.T, unit_block, precision=highest, preferred_element_type=jnp.float32)
        return (text_sums, image_part)
    text_grad, image_parts = lax.scan(block_step, jnp.zeros((BATCH, E), jnp.float32), (blocks, starts))
    image_grad = image_parts.reshape(BATCH, E)
    image_dz = image_inverse * (image_grad - image_unit * lax.optimization_barrier(jnp.sum(image_unit * image_grad, axis=1, keepdims=True)))
    text_dz = text_inverse * (text_grad - text_unit * lax.optimization_barrier(jnp.sum(text_unit * text_grad, axis=1, keepdims=True)))
    grad_image_features = jnp.dot(image_dz, image_proj.T, precision=highest, preferred_element_type=jnp.float32)
    grad_text_features = jnp.dot(text_dz, text_proj.T, precision=highest, preferred_element_type=jnp.float32)
    grad_image_proj = jnp.dot(image_features.T, image_dz, precision=highest, preferred_element_type=jnp.float32)
    grad_text_proj = jnp.dot(text_features.T, text_dz, precision=highest, preferred_element_type=jnp.float32)
    return (grad_image_features, grad_text_features, grad_image_proj, grad_text_proj)
```

```python
import jax
import jax.numpy as jnp
from jax import lax
from jax.sharding import Mesh, PartitionSpec as P

logit_scale = 100.0
logit_bias = -10.0
epsilon_norm = 1e-06
GROUP = ("xl", "core")
IMAGE_AXES = ("z", "core")
TEXT_AXES = ("y", "xh", "xl")


def dot(a, b, dims):
    return lax.dot_general(
        a, b, (dims, ((), ())), precision=lax.Precision.HIGH, preferred_element_type=jnp.float32
    )


def normalize(values):
    inverse = lax.rsqrt(jnp.sum(values * values, axis=-1, keepdims=True) + epsilon_norm)
    return (values * inverse, inverse)


def on_device(image_features, text_features, image_proj, text_proj):
    rows, width = image_features.shape
    group_image = lax.all_gather(image_features, GROUP, axis=0, tiled=True)
    group_text = lax.all_gather(text_features, GROUP, axis=0, tiled=True)
    cols = jnp.stack(
        [dot(group_image, image_proj, ((1,), (0,))), dot(group_text, text_proj, ((1,), (0,)))]
    )
    raw = lax.all_to_all(cols, GROUP, split_axis=1, concat_axis=2, tiled=True)
    unit, inverse = normalize(raw)
    images = lax.all_gather(unit[0], IMAGE_AXES, axis=0, tiled=True)
    texts = lax.all_gather(unit[1], TEXT_AXES, axis=0, tiled=True)
    image_first = lax.axis_index(IMAGE_AXES) * rows
    text_first = lax.axis_index(TEXT_AXES) * rows
    shape = (images.shape[0], texts.shape[0])
    i = lax.broadcasted_iota(jnp.int32, shape, 0) - image_first
    j = lax.broadcasted_iota(jnp.int32, shape, 1) - text_first
    target = jnp.where((i == j) & (i >= 0) & (i < rows), 1.0, 0.0)
    logits = logit_scale * dot(images, texts, ((1,), (1,))) + logit_bias
    pair_grad = jax.nn.sigmoid(logits) - target
    image_sum = logit_scale * dot(pair_grad, texts, ((1,), (0,)))
    text_sum = logit_scale * dot(pair_grad, images, ((0,), (0,)))
    image_grad = lax.psum_scatter(image_sum, IMAGE_AXES, scatter_dimension=0, tiled=True)
    text_grad = lax.psum_scatter(text_sum, TEXT_AXES, scatter_dimension=0, tiled=True)
    grad = jnp.stack([image_grad, text_grad])
    dz = inverse * (grad - unit * jnp.sum(unit * grad, axis=2, keepdims=True))
    dcols = lax.all_to_all(dz, GROUP, split_axis=2, concat_axis=1, tiled=True)
    image_weight = dot(group_image, dcols[0], ((0,), (0,)))
    text_weight = dot(group_text, dcols[1], ((0,), (0,)))
    weight = jnp.concatenate([image_weight, text_weight], axis=0)
    for axis in ("z", "y", "xh"):
        weight = lax.psum_scatter(weight, axis, scatter_dimension=0, tiled=True)
    image_part = dot(dcols[0], image_proj, ((1,), (1,)))
    text_part = dot(dcols[1], text_proj, ((1,), (1,)))
    combined = lax.psum_scatter(
        jnp.concatenate([image_part, text_part], axis=1), GROUP, scatter_dimension=0, tiled=True
    )
    for axis in ("xh", "y", "z"):
        weight = lax.all_gather(weight, axis, axis=0, tiled=True)
    return (combined[:, :width], combined[:, width:], weight[:width], weight[width:])


def solution(mesh):
    fine = Mesh(mesh.devices.reshape(8, 4, 2, 2, 2), ("z", "y", "xh", "xl", "core"))
    rows = P(("z", "y", "xh", "xl", "core"), None)
    cols = P(None, GROUP)
    return jax.shard_map(
        on_device,
        mesh=fine,
        in_specs=(rows, rows, cols, cols),
        out_specs=(rows, rows, cols, cols),
        check_vma=False,
    )
```

```python
import jax
import jax.numpy as jnp
from jax import lax
from jax.experimental import pallas as pl
from jax.experimental.pallas import tpu as pltpu
from jax.sharding import Mesh, PartitionSpec as P

logit_scale = 100.0
logit_bias = -10.0
epsilon_norm = 1e-06
NZ, NY, NX, NC = 8, 4, 4, 2
GROUP = ("xl", "core")
MESH = pl.DeviceIdType.MESH
COPIES = 96


class Net:
    def __init__(self, send, recv):
        self.send, self.recv = send, recv
        self.z, self.y, self.c = (lax.axis_index(a) for a in ("z", "y", "core"))
        self.x = lax.axis_index("xh") * 2 + lax.axis_index("xl")
        self.started = []

    def device(self, z=None, y=None, x=None, c=None):
        z, y, x, c = (
            mine if other is None else other
            for mine, other in ((self.z, z), (self.y, y), (self.x, x), (self.c, c))
        )
        return (z, y, x // 2, x % 2, c)

    def along(self, axis, step):
        size = {"z": NZ, "y": NY, "x": NX, "c": NC}[axis]
        return self.device(**{axis: (getattr(self, axis) + step + size) % size})

    def copy(self, src, dst, device):
        k = len(self.started)
        one = pltpu.make_async_remote_copy(
            src_ref=src, dst_ref=dst, send_sem=self.send.at[k], recv_sem=self.recv.at[k],
            device_id=device, device_id_type=MESH,
        )
        one.start()
        self.started.append(one)
        return one

    def barrier(self, devices):
        semaphore = pltpu.get_barrier_semaphore()
        for device in devices:
            pl.semaphore_signal(semaphore, inc=1, device_id=device, device_id_type=MESH)
        pl.semaphore_wait(semaphore, len(devices))

    def finish(self):
        for one in self.started:
            one.wait_send()


def interleave(streams):
    streams = list(streams)
    while streams:
        left = []
        for stream in streams:
            try:
                next(stream)
                left.append(stream)
            except StopIteration:
                pass
        streams = left


def ring_gather(net, axis, n, slot, length, landed=None):
    me = getattr(net, axis)
    half = n // 2
    cut = length // 2
    parts = (pl.ds(0, cut), pl.ds(cut, length - cut))
    previous = None
    for step in range(1, half + 1):
        now = []
        for way, sign in ((0, 1), (1, -1)):
            origin = slot((me - sign * (step - 1) + n) % n)
            if previous is not None:
                previous[way].wait_recv()
            if step == half:
                origin = origin.at[parts[way]]
            now.append(net.copy(origin, origin, net.along(axis, sign)))
        if previous is not None and landed is not None:
            landed(step - 1)
            landed(1 - step)
        previous = now
        yield
    for one in previous:
        one.wait_recv()
    if landed is not None:
        landed(half)


def ring_reduce(net, axis, n, src, length, from_left, from_right, out, ready=None):
    me = getattr(net, axis)
    half = n // 2
    cut = length // 2
    parts = (pl.ds(0, cut), pl.ds(cut, length - cut))
    arrived = (from_left, from_right)
    previous = None
    for step in range(1, half + 1):
        far = half - step + 1
        now = []
        for way, sign in ((0, 1), (1, -1)):
            if ready is not None and (step > 1 or way == 0):
                ready(sign * far)
            own = src((me + sign * far + n) % n)
            if step == 1:
                piece, place = own.at[parts[way]], arrived[way].at[0, parts[way]]
            else:
                previous[way].wait_recv()
                held = arrived[way].at[step - 2]
                if step == 2:
                    held[parts[way]] = held[parts[way]] + own[parts[way]]
                    held[parts[1 - way]] = own[parts[1 - way]]
                else:
                    held[...] = held[...] + own[...]
                piece, place = held, arrived[way].at[step - 1]
            now.append(net.copy(piece, place, net.along(axis, sign)))
        previous = now
        yield
    if ready is not None:
        ready(0)
    for one in previous:
        one.wait_recv()
    out(src(me)[...] + from_left[half - 1] + from_right[half - 1])


def neighbours(net):
    return [net.along(axis, step) for axis in "zyx" for step in (1, -1)]


def gather_kernel(unit, images, texts_a, texts_b, send, recv):
    net = Net(send, recv)
    net.barrier(neighbours(net) + [net.along("c", 1)])
    images[net.c, net.z] = unit[0]
    texts_a[net.y, net.x] = unit[1, 0:2]
    texts_b[net.x, net.y] = unit[1, 2:4]
    across = []

    def image_stream(first, length):
        def slot(z):
            return images.at[net.c, z, pl.ds(first, length)]

        def landed(relative):
            block = slot((net.z + relative + NZ) % NZ)
            across.append(net.copy(block, block, net.along("c", 1)))

        landed(0)
        yield from ring_gather(net, "z", NZ, slot, length, landed)

    def text_stream(buffer, first, second, counts):
        mine = getattr(net, first)
        other = getattr(net, second)
        row = buffer.at[other]
        yield from ring_gather(net, first, counts[0], lambda i: row.at[i], 2)
        yield from ring_gather(net, second, counts[1], lambda i: buffer.at[i], counts[0])

    interleave(
        [
            image_stream(0, 2),
            text_stream(texts_a, "x", "y", (NX, NY)),
            text_stream(texts_b, "y", "x", (NY, NX)),
            image_stream(2, 2),
        ]
    )
    for one in across:
        one.wait_recv()
    net.finish()


def reduce_kernel(images, texts_a, texts_b, image_out, text_out, sibling, z0, z1, a0, a1, a2, a3, a4,
                  b0, b1, b2, b3, b4, send, recv):
    net = Net(send, recv)
    net.barrier(neighbours(net) + [net.along("c", 1)])
    pending = {}
    for relative in (4, 3, -3, 2, -2, 1, -1, 0):
        z = (net.z + relative + NZ) % NZ
        pending[relative] = net.copy(images.at[1 - net.c, z], sibling.at[z], net.along("c", 1))

    def ready(relative):
        z = (net.z + relative + NZ) % NZ
        pending[relative].wait_recv()
        sibling[z] = sibling[z] + images[net.c, z]

    def image_done(total):
        image_out[...] = total

    def text_stream(buffer, first, second, counts, scratch, place):
        middle, l1, r1, l2, r2 = scratch

        def halfway(total):
            middle[...] = total

        def done(total):
            text_out[place] = total

        yield from ring_reduce(net, first, counts[0], lambda i: buffer.at[i], counts[1], l1, r1, halfway)
        yield from ring_reduce(net, second, counts[1], lambda i: middle.at[i], 2, l2, r2, done)

    interleave(
        [
            text_stream(texts_a, "y", "x", (NY, NX), (a0, a1, a2, a3, a4), pl.ds(0, 2)),
            text_stream(texts_b, "x", "y", (NX, NY), (b0, b1, b2, b3, b4), pl.ds(2, 2)),
            ring_reduce(net, "z", NZ, lambda i: sibling.at[i], 4, z0, z1, image_done, ready),
        ]
    )
    net.finish()


A_TILES = 320
B_TILES = 328
AZ, AY = A_TILES // NZ, A_TILES // NZ // NY
BY, BZ = B_TILES // NY, 11


def weight_kernel(part, total, a_mid, b_mid, a_own, b_own, a_pair, b_pair, a_all, b_all,
                  az0, az1, ay0, ay1, by0, by1, bz0, bz1, send, recv):
    net = Net(send, recv)
    partner = net.device(x=(net.x + 2) % NX)
    net.barrier([net.along(axis, step) for axis in "zy" for step in (1, -1)] + [partner])

    def store(ref, index=...):
        def put(value):
            ref[index] = value

        return put

    def pair_sum(own, pair, put):
        one = net.copy(own, pair, partner)
        yield
        one.wait_recv()
        put(own[...] + pair[...])

    def stream_a():
        yield from ring_reduce(
            net, "z", NZ, lambda i: part.at[pl.ds(i * AZ, AZ)], AZ, az0, az1, store(a_mid)
        )
        yield from ring_reduce(
            net, "y", NY, lambda i: a_mid.at[pl.ds(i * AY, AY)], AY, ay0, ay1, store(a_own)
        )
        yield from pair_sum(a_own, a_pair, store(a_all, pl.ds(net.y * AY, AY)))
        yield from ring_gather(net, "y", NY, lambda i: a_all.at[pl.ds(i * AY, AY)], AY)
        total[pl.ds(net.z * AZ, AZ)] = a_all[...]
        yield from ring_gather(net, "z", NZ, lambda i: total.at[pl.ds(i * AZ, AZ)], AZ)

    def stream_b():
        yield from ring_reduce(
            net, "y", NY, lambda i: part.at[pl.ds(A_TILES + i * BY, BY)], BY, by0, by1,
            store(b_mid, pl.ds(0, BY)),
        )
        b_mid[pl.ds(BY, NZ * BZ - BY)] = jnp.zeros((NZ * BZ - BY, 8, 128), jnp.float32)
        yield from ring_reduce(
            net, "z", NZ, lambda i: b_mid.at[pl.ds(i * BZ, BZ)], BZ, bz0, bz1, store(b_own)
        )
        yield from pair_sum(b_own, b_pair, store(b_all, pl.ds(net.z * BZ, BZ)))
        yield from ring_gather(net, "z", NZ, lambda i: b_all.at[pl.ds(i * BZ, BZ)], BZ)
        total[pl.ds(A_TILES + net.y * BY, BY)] = b_all[pl.ds(0, BY)]
        yield from ring_gather(
            net, "y", NY, lambda i: total.at[pl.ds(A_TILES + i * BY, BY)], BY
        )

    interleave([stream_a(), stream_b()])
    net.finish()


def call(kernel, outs, scratch, collective, *args):
    vmem = pl.BlockSpec(memory_space=pltpu.VMEM)
    return pl.pallas_call(
        kernel,
        out_shape=[jax.ShapeDtypeStruct(s, jnp.float32) for s in outs],
        in_specs=[vmem] * len(args),
        out_specs=[vmem] * len(outs),
        scratch_shapes=[pltpu.VMEM(s, jnp.float32) for s in scratch]
        + [pltpu.SemaphoreType.DMA((COPIES,))] * 2,
        compiler_params=pltpu.CompilerParams(
            collective_id=collective, has_side_effects=True, vmem_limit_bytes=40 * 2**20
        ),
    )(*args)


def gather_pairs(unit):
    width = unit.shape[-1]
    tiles = unit.reshape(2, 4, 8, width)
    outs = [(NC, NZ, 4, 8, width), (NY, NX, 2, 8, width), (NX, NY, 2, 8, width)]
    images, texts_a, texts_b = call(gather_kernel, outs, [], 1, tiles)
    texts = jnp.concatenate([texts_a.reshape(-1, width), texts_b.reshape(-1, width)], axis=0)
    return (images.reshape(-1, width), texts)


def reduce_pairs(image_sum, text_sum):
    width = image_sum.shape[-1]
    tile = (8, width)
    outs = [(4,) + tile, (4,) + tile]
    scratch = [(NZ, 4) + tile, (NZ // 2, 4) + tile, (NZ // 2, 4) + tile]
    for a, b in ((NY, NX), (NX, NY)):
        scratch += [(b, 2) + tile] + [(a // 2, b, 2) + tile] * 2 + [(b // 2, 2) + tile] * 2
    count = text_sum.shape[0] // 2
    image, text = call(
        reduce_kernel, outs, scratch, 2,
        image_sum.reshape((NC, NZ, 4) + tile),
        text_sum[:count].reshape((NY, NX, 2) + tile),
        text_sum[count:].reshape((NX, NY, 2) + tile),
    )
    return (image.reshape(32, width), text.reshape(32, width))


def reduce_weights(part):
    high, wide = part.shape
    tiles = part.reshape(high // 8, 8, wide // 128, 128).transpose(0, 2, 1, 3).reshape(-1, 8, 128)
    lengths = [AZ, NZ * BZ, AY, BZ, AY, BZ, AZ, NZ * BZ]
    scratch = [(n, 8, 128) for n in lengths]
    scratch += [(NZ // 2, AZ, 8, 128)] * 2 + [(NY // 2, AY, 8, 128)] * 2
    scratch += [(NY // 2, BY, 8, 128)] * 2 + [(NZ // 2, BZ, 8, 128)] * 2
    (total,) = call(weight_kernel, [tiles.shape], scratch, 3, tiles)
    return total.reshape(high // 8, wide // 128, 8, 128).transpose(0, 2, 1, 3).reshape(high, wide)


def dot(a, b, dims):
    return lax.dot_general(
        a, b, (dims, ((), ())), precision=lax.Precision.HIGH, preferred_element_type=jnp.float32
    )


def normalize(values):
    inverse = lax.rsqrt(jnp.sum(values * values, axis=-1, keepdims=True) + epsilon_norm)
    return (values * inverse, inverse)


def pair_target(rows):
    z, y, c = (lax.axis_index(a) for a in ("z", "y", "core"))
    x = lax.axis_index("xh") * 2 + lax.axis_index("xl")
    i = lax.broadcasted_iota(jnp.int32, (16 * rows, 16 * rows), 0) - (c * NZ + z) * rows
    j = lax.broadcasted_iota(jnp.int32, (16 * rows, 16 * rows), 1)
    half, count = rows // 2, 8 * rows
    a = j - (y * NX + x) * half
    b = j - count - (x * NY + y) * half + half
    same_a = (i == a) & (a >= 0) & (a < half)
    same_b = (i == b) & (b >= half) & (b < rows)
    return jnp.where(same_a | same_b, 1.0, 0.0)


def on_device(image_features, text_features, image_proj, text_proj):
    rows, width = image_features.shape
    group_image = lax.all_gather(image_features, GROUP, axis=0, tiled=True)
    group_text = lax.all_gather(text_features, GROUP, axis=0, tiled=True)
    cols = jnp.stack(
        [dot(group_image, image_proj, ((1,), (0,))), dot(group_text, text_proj, ((1,), (0,)))]
    )
    raw = lax.all_to_all(cols, GROUP, split_axis=1, concat_axis=2, tiled=True)
    unit, inverse = normalize(raw)
    images, texts = gather_pairs(unit)
    logits = logit_scale * dot(images, texts, ((1,), (1,))) + logit_bias
    pair_grad = jax.nn.sigmoid(logits) - pair_target(rows)
    image_sum = logit_scale * dot(pair_grad, texts, ((1,), (0,)))
    text_sum = logit_scale * dot(pair_grad, images, ((0,), (0,)))
    grad = jnp.stack(reduce_pairs(image_sum, text_sum))
    dz = inverse * (grad - unit * jnp.sum(unit * grad, axis=2, keepdims=True))
    dcols = lax.all_to_all(dz, GROUP, split_axis=2, concat_axis=1, tiled=True)
    image_weight = dot(dcols[0], group_image, ((0,), (0,)))
    text_weight = dot(dcols[1], group_text, ((0,), (0,)))
    weight = reduce_weights(jnp.concatenate([image_weight, text_weight], axis=0))
    image_part = dot(dcols[0], image_proj, ((1,), (1,)))
    text_part = dot(dcols[1], text_proj, ((1,), (1,)))
    combined = lax.psum_scatter(
        jnp.concatenate([image_part, text_part], axis=1), GROUP, scatter_dimension=0, tiled=True
    )
    columns = image_proj.shape[1]
    return (combined[:, :width], combined[:, width:], weight[:columns].T, weight[columns:].T)


def solution(mesh):
    fine = Mesh(mesh.devices.reshape(NZ, NY, 2, 2, NC), ("z", "y", "xh", "xl", "core"))
    rows = P(("z", "y", "xh", "xl", "core"), None)
    cols = P(None, GROUP)
    return jax.shard_map(
        on_device,
        mesh=fine,
        in_specs=(rows, rows, cols, cols),
        out_specs=(rows, rows, cols, cols),
        check_vma=False,
    )
```

```python
import jax
import jax.numpy as jnp
from jax import lax
from jax.experimental import pallas as pl
from jax.experimental.pallas import tpu as pltpu
from jax.sharding import Mesh, PartitionSpec as P

logit_scale = 100.0
logit_bias = -10.0
epsilon_norm = 1e-06
NZ, NY, NX, NC = 8, 4, 4, 2
GROUP = ("xl", "core")
MESH = pl.DeviceIdType.MESH
COPIES = 176


class Net:
    def __init__(self, send, recv):
        self.send, self.recv = send, recv
        self.z, self.y, self.c = (lax.axis_index(a) for a in ("z", "y", "core"))
        self.x = lax.axis_index("xh") * 2 + lax.axis_index("xl")
        self.started = []

    def device(self, z=None, y=None, x=None, c=None):
        z, y, x, c = (
            mine if other is None else other
            for mine, other in ((self.z, z), (self.y, y), (self.x, x), (self.c, c))
        )
        return (z, y, x // 2, x % 2, c)

    def along(self, axis, step):
        size = {"z": NZ, "y": NY, "x": NX, "c": NC}[axis]
        return self.device(**{axis: (getattr(self, axis) + step + size) % size})

    def copy(self, src, dst, device):
        k = len(self.started)
        one = pltpu.make_async_remote_copy(
            src_ref=src, dst_ref=dst, send_sem=self.send.at[k], recv_sem=self.recv.at[k],
            device_id=device, device_id_type=MESH,
        )
        one.start()
        self.started.append(one)
        return one

    def barrier(self, devices):
        semaphore = pltpu.get_barrier_semaphore()
        for device in devices:
            pl.semaphore_signal(semaphore, inc=1, device_id=device, device_id_type=MESH)
        pl.semaphore_wait(semaphore, len(devices))

    def finish(self):
        for one in self.started:
            one.wait_send()


def interleave(streams):
    streams = list(streams)
    while streams:
        left = []
        for stream in streams:
            try:
                next(stream)
                left.append(stream)
            except StopIteration:
                pass
        streams = left


def ring_gather(net, axis, n, slot, length, landed=None):
    me = getattr(net, axis)
    half = n // 2
    cut = length // 2
    parts = (pl.ds(0, cut), pl.ds(cut, length - cut))
    previous = None
    for step in range(1, half + 1):
        now = []
        for way, sign in ((0, 1), (1, -1)):
            origin = slot((me - sign * (step - 1) + n) % n)
            if previous is not None:
                previous[way].wait_recv()
            if step == half:
                origin = origin.at[parts[way]]
            now.append(net.copy(origin, origin, net.along(axis, sign)))
        if previous is not None and landed is not None:
            landed(step - 1)
            landed(1 - step)
        previous = now
        yield
    for one in previous:
        one.wait_recv()
    if landed is not None:
        landed(half)


def ring_reduce(net, axis, n, src, length, from_left, from_right, out, ready=None):
    me = getattr(net, axis)
    half = n // 2
    cut = length // 2
    parts = (pl.ds(0, cut), pl.ds(cut, length - cut))
    arrived = (from_left, from_right)
    previous = None
    for step in range(1, half + 1):
        far = half - step + 1
        now = []
        for way, sign in ((0, 1), (1, -1)):
            if ready is not None and (step > 1 or way == 0):
                ready(sign * far)
            own = src((me + sign * far + n) % n)
            if step == 1:
                piece, place = own.at[parts[way]], arrived[way].at[0, parts[way]]
            else:
                previous[way].wait_recv()
                held = arrived[way].at[step - 2]
                if step == 2:
                    held[parts[way]] = held[parts[way]] + own[parts[way]]
                    held[parts[1 - way]] = own[parts[1 - way]]
                else:
                    held[...] = held[...] + own[...]
                piece, place = held, arrived[way].at[step - 1]
            now.append(net.copy(piece, place, net.along(axis, sign)))
        previous = now
        yield
    if ready is not None:
        ready(0)
    for one in previous:
        one.wait_recv()
    out(src(me)[...] + from_left[half - 1] + from_right[half - 1])


def neighbours(net):
    return [net.along(axis, step) for axis in "zyx" for step in (1, -1)]


def group_places(net):
    low, high = net.x % 2, net.x - net.x % 2
    here = (low * 2 + net.c, low * 2 + 1 - net.c)
    there = ((1 - low) * 2 + net.c, (1 - low) * 2 + 1 - net.c)
    other = high + 1 - low
    devices = (net.device(c=1 - net.c), net.device(x=other), net.device(x=other, c=1 - net.c))
    return here + there, devices


def greet(net):
    _, (_, _, diagonal) = group_places(net)
    net.barrier(neighbours(net) + [net.along("c", 1), diagonal])


def halves(value):
    high = value.astype(jnp.bfloat16)
    return (high, (value - high.astype(jnp.float32)).astype(jnp.bfloat16))


def dot3(a, b, dims):
    def one(p, q):
        return lax.dot_general(p, q, (dims, ((), ())), preferred_element_type=jnp.float32)

    return one(a[0], b[0]) + (one(a[0], b[1]) + one(a[1], b[0]))


def front_kernel(image_x, text_x, image_w, text_w, images, texts, group, unit, inverse,
                 col_out, col_in, send, recv):
    net = Net(send, recv)
    (me, sib, far, diag), (to_sib, to_far, to_diag) = group_places(net)
    rows, width = image_x.shape
    part = image_w.shape[1]
    greet(net)
    group[0, me] = image_x[...]
    group[1, me] = text_x[...]
    first = []
    for t in range(2):
        block = group.at[t, me]
        first.append((net.copy(block, block, to_far), net.copy(block, block, to_sib)))
    across = []

    def prepare(t, w):
        weights = halves(w[...])
        first[t][0].wait_recv()
        block = group.at[t, far]
        onward = net.copy(block, block, to_sib)
        yield
        first[t][1].wait_recv()
        onward.wait_recv()
        cols = dot3(halves(group[t].reshape(4 * rows, width)), weights, ((1,), (0,)))
        col_out[t] = cols.reshape(4, rows, part)
        copies = [
            net.copy(col_out.at[t, place], col_in.at[t, me], device)
            for place, device in ((far, to_far), (diag, to_diag), (sib, to_sib))
        ]
        col_in[t, me] = col_out[t, me]
        yield
        for one in copies:
            one.wait_recv()
        raw = jnp.concatenate([col_in[t, k] for k in range(4)], axis=1)
        scale = lax.rsqrt(jnp.sum(raw * raw, axis=1, keepdims=True) + epsilon_norm)
        unit[t] = raw * scale
        inverse[t] = jnp.broadcast_to(scale, (rows, 128))

    def image_start():
        yield from prepare(0, image_w)
        images[net.c, net.z] = unit[0].reshape(4, 8, width)

    def text_start():
        yield from prepare(1, text_w)
        tiles = unit[1].reshape(4, 8, width)
        texts[0, net.y, net.x] = tiles[0:2]
        texts[1, net.x, net.y] = tiles[2:4]

    def image_stream(first, length):
        def slot(z):
            return images.at[net.c, z, pl.ds(first, length)]

        def landed(relative):
            block = slot((net.z + relative + NZ) % NZ)
            across.append(net.copy(block, block, net.along("c", 1)))

        yield from ring_gather(net, "z", NZ, slot, length, landed)

    def text_stream(half, first, second, counts):
        buffer = texts.at[half]
        row = buffer.at[getattr(net, second)]
        yield from ring_gather(net, first, counts[0], lambda i: row.at[i], 2)
        yield from ring_gather(net, second, counts[1], lambda i: buffer.at[i], counts[0])

    interleave([image_start(), text_start()])
    own = images.at[net.c, net.z]
    streams = [
        image_stream(0, 2),
        text_stream(0, "x", "y", (NX, NY)),
        text_stream(1, "y", "x", (NY, NX)),
        image_stream(2, 2),
    ]
    for stream in streams:
        next(stream)
    across.append(net.copy(own, own, net.along("c", 1)))
    interleave(streams)
    for one in across:
        one.wait_recv()
    net.finish()


A_STREAMS, B_STREAMS = 2, 2
AZ, AY = 20, 5
BY, BZ = 41, 6
A_TILES = A_STREAMS * NZ * AZ


def weight_stream_a(net, partner, base, part, total, mid, own, pair, every, z0, z1, y0, y1):
    def put(ref, index=...):
        def store(value):
            ref[index] = value

        return store

    yield from ring_reduce(
        net, "z", NZ, lambda i: part.at[pl.ds(base + i * AZ, AZ)], AZ, z0, z1, put(mid)
    )
    yield from ring_reduce(net, "y", NY, lambda i: mid.at[pl.ds(i * AY, AY)], AY, y0, y1, put(own))
    one = net.copy(own, pair, partner)
    yield
    one.wait_recv()
    every[pl.ds(net.y * AY, AY)] = own[...] + pair[...]
    yield from ring_gather(net, "y", NY, lambda i: every.at[pl.ds(i * AY, AY)], AY)
    total[pl.ds(base + net.z * AZ, AZ)] = every[...]
    yield from ring_gather(net, "z", NZ, lambda i: total.at[pl.ds(base + i * AZ, AZ)], AZ)


def weight_stream_b(net, partner, base, part, total, mid, own, pair, every, y0, y1, z0, z1):
    def put(ref, index=...):
        def store(value):
            ref[index] = value

        return store

    mid[pl.ds(BY, NZ * BZ - BY)] = jnp.zeros((NZ * BZ - BY, 8, 128), jnp.float32)
    yield from ring_reduce(
        net, "y", NY, lambda i: part.at[pl.ds(base + i * BY, BY)], BY, y0, y1, put(mid, pl.ds(0, BY))
    )
    yield from ring_reduce(net, "z", NZ, lambda i: mid.at[pl.ds(i * BZ, BZ)], BZ, z0, z1, put(own))
    one = net.copy(own, pair, partner)
    yield
    one.wait_recv()
    every[pl.ds(net.z * BZ, BZ)] = own[...] + pair[...]
    yield from ring_gather(net, "z", NZ, lambda i: every.at[pl.ds(i * BZ, BZ)], BZ)
    total[pl.ds(base + net.y * BY, BY)] = every[pl.ds(0, BY)]
    yield from ring_gather(net, "y", NY, lambda i: total.at[pl.ds(base + i * BY, BY)], BY)


def back_shapes(width, part):
    tile, small = (8, width), (8, 128)
    rows = 32
    shapes = [(NZ, 4) + tile]
    shapes += [(NZ // 2, 2) + tile] * 4
    for a, b in ((NY, NX), (NX, NY)):
        shapes += [(b, 2) + tile] + [(a // 2, b, 2) + tile] * 2 + [(b // 2, 2) + tile] * 2
    shapes += [(2, 4) + tile]
    shapes += [(2, 4, rows, part)] * 2
    shapes += [(2 * part // 8 * (width // 128),) + small]
    shapes += [(2, 4, rows, width), (2, 2, rows, width), (2, rows, width)]
    for _ in range(A_STREAMS):
        shapes += [(n,) + small for n in (AZ, AY, AY, AZ)]
        shapes += [(NZ // 2, AZ) + small] * 2 + [(NY // 2, AY) + small] * 2
    for _ in range(B_STREAMS):
        shapes += [(n,) + small for n in (NZ * BZ, BZ, BZ, NZ * BZ)]
        shapes += [(NY // 2, BY) + small] * 2 + [(NZ // 2, BZ) + small] * 2
    return shapes


def back_kernel(images, texts, unit, inverse, group, image_w, text_w, image_out, text_out, total,
                sibling, *rest):
    send, recv = rest[-2:]
    rest = list(rest[:-2])

    def take(count):
        taken = rest[:count]
        del rest[:count]
        return taken

    z_low, z_high = take(2), take(2)
    text_scratch = (take(5), take(5))
    grad, d_out, d_in, part, feature, feature_in, feature_sum = take(7)
    a_scratch = [take(8) for _ in range(A_STREAMS)]
    b_scratch = [take(8) for _ in range(B_STREAMS)]
    net = Net(send, recv)
    (me, sib, far, diag), (to_sib, to_far, to_diag) = group_places(net)
    partner = net.device(x=(net.x + 2) % NX)
    rows, width = image_out.shape
    columns = image_w.shape[1]
    semaphores = [net.device(x=(net.x + 2) % NX)]
    _, (_, _, diagonal) = group_places(net)
    net.barrier(neighbours(net) + [net.along("c", 1), diagonal] + semaphores)
    pending = {}
    order = (4, 3, -3, 2, -2, 1, -1, 0)
    for relative in order:
        z = (net.z + relative + NZ) % NZ
        pending[relative] = net.copy(images.at[1 - net.c, z], sibling.at[z], net.along("c", 1))
    summed = set()

    def ready(relative):
        if relative in summed:
            return
        summed.add(relative)
        z = (net.z + relative + NZ) % NZ
        pending[relative].wait_recv()
        sibling[z] = sibling[z] + images[net.c, z]

    def put(ref, *index):
        def store(value):
            ref[index] = value

        return store

    def image_stream(first, scratch):
        yield from ring_reduce(
            net, "z", NZ, lambda i: sibling.at[i, pl.ds(first, 2)], 2, *scratch,
            put(grad, 0, pl.ds(first, 2)), ready,
        )

    def text_stream(half, first, second, counts, scratch):
        buffer = texts.at[half]
        middle, l1, r1, l2, r2 = scratch
        yield from ring_reduce(
            net, first, counts[0], lambda i: buffer.at[i], counts[1], l1, r1, put(middle, ...)
        )
        yield from ring_reduce(
            net, second, counts[1], lambda i: middle.at[i], 2, l2, r2,
            put(grad, 1, pl.ds(half * 2, 2)),
        )

    interleave(
        [
            image_stream(0, z_low),
            text_stream(0, "y", "x", (NY, NX), text_scratch[0]),
            text_stream(1, "x", "y", (NX, NY), text_scratch[1]),
            image_stream(2, z_high),
        ]
    )

    exchanged = []
    for t in range(2):
        g, u = grad[t].reshape(rows, width), unit[t]
        dz = inverse[t][:, :1] * (g - u * jnp.sum(u * g, axis=1, keepdims=True))
        for k in range(4):
            d_out[t, k] = dz[:, k * columns : (k + 1) * columns]
        exchanged.append(
            [
                net.copy(d_out.at[t, place], d_in.at[t, me], device)
                for place, device in ((far, to_far), (diag, to_diag), (sib, to_sib))
            ]
        )
        d_in[t, me] = d_out[t, me]

    per_tower = columns // 8
    lanes = width // 128
    feature_first = []
    for t, w in ((0, image_w), (1, text_w)):
        for one in exchanged[t]:
            one.wait_recv()
        dcols = halves(d_in[t].reshape(4 * rows, columns))
        x = halves(group[t].reshape(4 * rows, width))
        weight = dot3(dcols, x, ((0,), (0,)))
        for j in range(lanes):
            part[pl.ds((t * lanes + j) * per_tower, per_tower)] = weight[
                :, j * 128 : (j + 1) * 128
            ].reshape(per_tower, 8, 128)

    def feature_stream():
        for t, w in ((0, image_w), (1, text_w)):
            dcols = halves(d_in[t].reshape(4 * rows, columns))
            terms = dot3(dcols, halves(w[...]), ((1,), (1,)))
            feature[t] = terms.reshape(4, rows, width)
            feature_first.append(
                (
                    net.copy(feature.at[t, diag], feature_in.at[t, 0], to_sib),
                    net.copy(feature.at[t, sib], feature_in.at[t, 1], to_sib),
                )
            )
        yield
        last = []
        for t in range(2):
            feature_first[t][0].wait_recv()
            feature_in[t, 0] = feature_in[t, 0] + feature[t, far]
            last.append(net.copy(feature_in.at[t, 0], feature_sum.at[t], to_far))
        for _ in range(6):
            yield
        for t, out in ((0, image_out), (1, text_out)):
            feature_first[t][1].wait_recv()
            last[t].wait_recv()
            out[...] = feature[t, me] + feature_in[t, 1] + feature_sum[t]

    streams = []
    for k in range(max(A_STREAMS, B_STREAMS)):
        if k < A_STREAMS:
            streams.append(
                weight_stream_a(net, partner, k * NZ * AZ, part, total, *a_scratch[k])
            )
        if k < B_STREAMS:
            streams.append(
                weight_stream_b(net, partner, A_TILES + k * NY * BY, part, total, *b_scratch[k])
            )
    interleave(streams + [feature_stream()])
    net.finish()


def call(kernel, outs, scratch, collective, *args):
    vmem = pl.BlockSpec(memory_space=pltpu.VMEM)
    return pl.pallas_call(
        kernel,
        out_shape=[jax.ShapeDtypeStruct(s, jnp.float32) for s in outs],
        in_specs=[vmem] * len(args),
        out_specs=[vmem] * len(outs),
        scratch_shapes=[pltpu.VMEM(s, jnp.float32) for s in scratch]
        + [pltpu.SemaphoreType.DMA((COPIES,))] * 2,
        compiler_params=pltpu.CompilerParams(
            collective_id=collective, has_side_effects=True, vmem_limit_bytes=52 * 2**20
        ),
    )(*args)


def dot(a, b, dims):
    return lax.dot_general(
        a, b, (dims, ((), ())), precision=lax.Precision.HIGH, preferred_element_type=jnp.float32
    )


def pair_target(rows):
    z, y, c = (lax.axis_index(a) for a in ("z", "y", "core"))
    x = lax.axis_index("xh") * 2 + lax.axis_index("xl")
    i = lax.broadcasted_iota(jnp.int32, (16 * rows, 16 * rows), 0) - (c * NZ + z) * rows
    j = lax.broadcasted_iota(jnp.int32, (16 * rows, 16 * rows), 1)
    half, count = rows // 2, 8 * rows
    a = j - (y * NX + x) * half
    b = j - count - (x * NY + y) * half + half
    same_a = (i == a) & (a >= 0) & (a < half)
    same_b = (i == b) & (b >= half) & (b < rows)
    return jnp.where(same_a | same_b, 1.0, 0.0)


def on_device(image_features, text_features, image_proj, text_proj):
    rows, width = image_features.shape
    columns = image_proj.shape[1]
    tile = (8, width)
    image_shape, text_shape = (NC, NZ, 4) + tile, (2, NY, NX, 2) + tile
    images, texts, group, unit, inverse = call(
        front_kernel,
        [image_shape, text_shape, (2, 4, rows, width), (2, rows, width), (2, rows, 128)],
        [(2, 4, rows, columns)] * 2, 1, image_features, text_features, image_proj, text_proj,
    )
    images, texts = images.reshape(-1, width), texts.reshape(-1, width)
    logits = logit_scale * dot(images, texts, ((1,), (1,))) + logit_bias
    pair_grad = jax.nn.sigmoid(logits) - pair_target(rows)
    image_sum = logit_scale * dot(pair_grad, texts, ((1,), (0,)))
    text_sum = logit_scale * dot(pair_grad, images, ((0,), (0,)))
    total_shape = (2 * columns // 8 * (width // 128), 8, 128)
    grad_image, grad_text, total = call(
        back_kernel, [(rows, width), (rows, width), total_shape], back_shapes(width, columns), 2,
        image_sum.reshape(image_shape), text_sum.reshape(text_shape), unit, inverse, group,
        image_proj, text_proj,
    )
    weights = total.reshape(2, width // 128, columns // 8, 8, 128).transpose(0, 1, 4, 2, 3)
    weights = weights.reshape(2, width, columns)
    return (grad_image, grad_text, weights[0], weights[1])


def solution(mesh):
    fine = Mesh(mesh.devices.reshape(NZ, NY, 2, 2, NC), ("z", "y", "xh", "xl", "core"))
    rows = P(("z", "y", "xh", "xl", "core"), None)
    cols = P(None, GROUP)
    return jax.shard_map(
        on_device,
        mesh=fine,
        in_specs=(rows, rows, cols, cols),
        out_specs=(rows, rows, cols, cols),
        check_vma=False,
    )
```

```python
import functools

import jax
import jax.numpy as jnp
from jax import lax
from jax.experimental import pallas as pl
from jax.experimental.pallas import tpu as pltpu
from jax.sharding import Mesh, PartitionSpec as P

logit_scale = 100.0
logit_bias = -10.0
epsilon_norm = 1e-06
NZ, NY, NX, NC = 8, 4, 4, 2
GROUP = ("xl", "core")
MESH = pl.DeviceIdType.MESH
COPIES = 256


class Net:
    def __init__(self, send, recv):
        self.send, self.recv = send, recv
        self.z, self.y, self.c = (lax.axis_index(a) for a in ("z", "y", "core"))
        self.x = lax.axis_index("xh") * 2 + lax.axis_index("xl")
        self.started = []

    def device(self, z=None, y=None, x=None, c=None):
        z, y, x, c = (
            mine if other is None else other
            for mine, other in ((self.z, z), (self.y, y), (self.x, x), (self.c, c))
        )
        return (z, y, x // 2, x % 2, c)

    def along(self, axis, step):
        size = {"z": NZ, "y": NY, "x": NX, "c": NC}[axis]
        return self.device(**{axis: (getattr(self, axis) + step + size) % size})

    def copy(self, src, dst, device):
        k = len(self.started)
        one = pltpu.make_async_remote_copy(
            src_ref=src, dst_ref=dst, send_sem=self.send.at[k], recv_sem=self.recv.at[k],
            device_id=device, device_id_type=MESH,
        )
        one.start()
        self.started.append(one)
        return one

    def barrier(self, devices):
        semaphore = pltpu.get_barrier_semaphore()
        for device in devices:
            pl.semaphore_signal(semaphore, inc=1, device_id=device, device_id_type=MESH)
        pl.semaphore_wait(semaphore, len(devices))

    def finish(self):
        for one in self.started:
            one.wait_send()


def interleave(streams):
    streams = list(streams)
    while streams:
        left = []
        for stream in streams:
            try:
                next(stream)
                left.append(stream)
            except StopIteration:
                pass
        streams = left


def ring_gather(net, axis, n, slot, length, landed=None):
    me = getattr(net, axis)
    half = n // 2
    cut = length // 2
    parts = (pl.ds(0, cut), pl.ds(cut, length - cut))
    previous = None
    for step in range(1, half + 1):
        now = []
        for way, sign in ((0, 1), (1, -1)):
            origin = slot((me - sign * (step - 1) + n) % n)
            if previous is not None:
                previous[way].wait_recv()
            if step == half:
                origin = origin.at[parts[way]]
            now.append(net.copy(origin, origin, net.along(axis, sign)))
        if previous is not None and landed is not None:
            landed(step - 1)
            landed(1 - step)
        previous = now
        yield
    for one in previous:
        one.wait_recv()
    if landed is not None:
        landed(half)


def ring_reduce(net, axis, n, src, length, from_left, from_right, out, ready=None):
    me = getattr(net, axis)
    half = n // 2
    cut = length // 2
    parts = (pl.ds(0, cut), pl.ds(cut, length - cut))
    arrived = (from_left, from_right)
    previous = None
    for step in range(1, half + 1):
        far = half - step + 1
        now = []
        for way, sign in ((0, 1), (1, -1)):
            if ready is not None and (step > 1 or way == 0):
                ready(sign * far)
            own = src((me + sign * far + n) % n)
            if step == 1:
                piece, place = own.at[parts[way]], arrived[way].at[0, parts[way]]
            else:
                previous[way].wait_recv()
                held = arrived[way].at[step - 2]
                if step == 2:
                    held[parts[way]] = held[parts[way]] + own[parts[way]]
                    held[parts[1 - way]] = own[parts[1 - way]]
                else:
                    held[...] = held[...] + own[...]
                piece, place = held, arrived[way].at[step - 1]
            now.append(net.copy(piece, place, net.along(axis, sign)))
        previous = now
        yield
    if ready is not None:
        ready(0)
    for one in previous:
        one.wait_recv()
    out(src(me)[...] + from_left[half - 1] + from_right[half - 1])


def neighbours(net):
    return [net.along(axis, step) for axis in "zyx" for step in (1, -1)]


def group_places(net):
    low, high = net.x % 2, net.x - net.x % 2
    here = (low * 2 + net.c, low * 2 + 1 - net.c)
    there = ((1 - low) * 2 + net.c, (1 - low) * 2 + 1 - net.c)
    other = high + 1 - low
    devices = (net.device(c=1 - net.c), net.device(x=other), net.device(x=other, c=1 - net.c))
    return here + there, devices


def halves(value):
    high = value.astype(jnp.bfloat16)
    return (high, (value - high.astype(jnp.float32)).astype(jnp.bfloat16))


def dot3(a, b, dims):
    def one(p, q):
        return lax.dot_general(p, q, (dims, ((), ())), preferred_element_type=jnp.float32)

    return one(a[0], b[0]) + (one(a[0], b[1]) + one(a[1], b[0]))


A_STREAMS, B_STREAMS = 2, 2
AZ, AY = 20, 5
BY, BZ = 41, 6
A_TILES = A_STREAMS * NZ * AZ


def weight_stream_a(net, partner, base, part, total, mid, own, pair, every, z0, z1, y0, y1):
    def put(ref, index=...):
        def store(value):
            ref[index] = value

        return store

    yield from ring_reduce(
        net, "z", NZ, lambda i: part.at[pl.ds(base + i * AZ, AZ)], AZ, z0, z1, put(mid)
    )
    yield from ring_reduce(net, "y", NY, lambda i: mid.at[pl.ds(i * AY, AY)], AY, y0, y1, put(own))
    one = net.copy(own, pair, partner)
    yield
    one.wait_recv()
    every[pl.ds(net.y * AY, AY)] = own[...] + pair[...]
    yield from ring_gather(net, "y", NY, lambda i: every.at[pl.ds(i * AY, AY)], AY)
    total[pl.ds(base + net.z * AZ, AZ)] = every[...]
    yield from ring_gather(net, "z", NZ, lambda i: total.at[pl.ds(base + i * AZ, AZ)], AZ)


def weight_stream_b(net, partner, base, part, total, mid, own, pair, every, y0, y1, z0, z1):
    def put(ref, index=...):
        def store(value):
            ref[index] = value

        return store

    mid[pl.ds(BY, NZ * BZ - BY)] = jnp.zeros((NZ * BZ - BY, 8, 128), jnp.float32)
    yield from ring_reduce(
        net, "y", NY, lambda i: part.at[pl.ds(base + i * BY, BY)], BY, y0, y1, put(mid, pl.ds(0, BY))
    )
    yield from ring_reduce(net, "z", NZ, lambda i: mid.at[pl.ds(i * BZ, BZ)], BZ, z0, z1, put(own))
    one = net.copy(own, pair, partner)
    yield
    one.wait_recv()
    every[pl.ds(net.z * BZ, BZ)] = own[...] + pair[...]
    yield from ring_gather(net, "z", NZ, lambda i: every.at[pl.ds(i * BZ, BZ)], BZ)
    total[pl.ds(base + net.y * BY, BY)] = every[pl.ds(0, BY)]
    yield from ring_gather(net, "y", NY, lambda i: total.at[pl.ds(base + i * BY, BY)], BY)


def scratch_shapes(rows, width, part):
    tile, small = (8, width), (8, 128)
    full = 16 * rows
    f, h = jnp.float32, jnp.bfloat16
    shapes = {
        "w": ((2, part, width), f),
        "images": ((NC, NZ, 4) + tile, f),
        "texts": ((2, NY, NX, 2) + tile, f),
        "group": ((2, 4, rows, width), f),
        "unit": ((2, rows, width), f),
        "inverse": ((2, rows, 128), f),
        "col_out": ((2, 4, rows, part), f),
        "col_in": ((2, 4, rows, part), f),
        "image_hi": ((full, width), h),
        "image_lo": ((full, width), h),
        "text_hi": ((full, width), h),
        "text_lo": ((full, width), h),
        "image_sum": ((NC, NZ, 4) + tile, f),
        "text_sum": ((2, NY, NX, 2) + tile, f),
        "sibling": ((NZ, 4) + tile, f),
    }
    for k in range(2):
        for way in "lr":
            shapes["z%d%s" % (k, way)] = ((NZ // 2, 2) + tile, f)
    for k, (m, n) in enumerate(((NY, NX), (NX, NY))):
        shapes["t%dm" % k] = ((n, 2) + tile, f)
        for way in "lr":
            shapes["t%d1%s" % (k, way)] = ((m // 2, n, 2) + tile, f)
            shapes["t%d2%s" % (k, way)] = ((n // 2, 2) + tile, f)
    shapes["grad"] = ((2, 4) + tile, f)
    shapes["d_out"] = ((2, 4, rows, part), f)
    shapes["d_in"] = ((2, 4, rows, part), f)
    shapes["weight"] = ((part, width), f)
    shapes["terms"] = ((2 * part // 8 * (width // 128),) + small, f)
    shapes["feature"] = ((2, 4, rows, width), f)
    shapes["feature_in"] = ((2, 2, rows, width), f)
    shapes["feature_sum"] = ((2, rows, width), f)
    for k in range(A_STREAMS):
        for name, count in zip(("mid", "own", "pair", "every"), (AZ, AY, AY, AZ)):
            shapes["a%d%s" % (k, name)] = ((count,) + small, f)
        for name, shape in (("z", (NZ // 2, AZ)), ("y", (NY // 2, AY))):
            for way in "lr":
                shapes["a%d%s%s" % (k, name, way)] = (shape + small, f)
    for k in range(B_STREAMS):
        for name, count in zip(("mid", "own", "pair", "every"), (NZ * BZ, BZ, BZ, NZ * BZ)):
            shapes["b%d%s" % (k, name)] = ((count,) + small, f)
        for name, shape in (("y", (NY // 2, BY)), ("z", (NZ // 2, BZ))):
            for way in "lr":
                shapes["b%d%s%s" % (k, name, way)] = (shape + small, f)
    return shapes


def kernel(names, image_x, text_x, image_w, text_w, image_out, text_out, total, *scratch):
    s = dict(zip(names, scratch))
    send, recv, load = scratch[len(names) :]
    images, texts, group, unit, inverse = (
        s[n] for n in ("images", "texts", "group", "unit", "inverse")
    )
    net = Net(send, recv)
    (me, sib, far, diag), (to_sib, to_far, to_diag) = group_places(net)
    partner = net.device(x=(net.x + 2) % NX)
    rows, width = image_x.shape
    part = image_w.shape[0]

    loads = [pltpu.make_async_copy(w, s["w"].at[t], load.at[t]) for t, w in ((0, image_w), (1, text_w))]
    for one in loads:
        one.start()
    group[0, me] = image_x[...]
    group[1, me] = text_x[...]
    net.barrier(neighbours(net) + [to_sib, to_diag, partner])

    first = []
    for t in range(2):
        block = group.at[t, me]
        first.append((net.copy(block, block, to_far), net.copy(block, block, to_sib)))
    across = []

    def prepare(t):
        loads[t].wait()
        weights = halves(s["w"][t])
        first[t][0].wait_recv()
        block = group.at[t, far]
        onward = net.copy(block, block, to_sib)
        yield
        first[t][1].wait_recv()
        onward.wait_recv()
        cols = dot3(halves(group[t].reshape(4 * rows, width)), weights, ((1,), (1,)))
        s["col_out"][t] = cols.reshape(4, rows, part)
        copies = [
            net.copy(s["col_out"].at[t, place], s["col_in"].at[t, me], device)
            for place, device in ((far, to_far), (diag, to_diag), (sib, to_sib))
        ]
        s["col_in"][t, me] = s["col_out"][t, me]
        yield
        for one in copies:
            one.wait_recv()
        raw = jnp.concatenate([s["col_in"][t, k] for k in range(4)], axis=1)
        scale = lax.rsqrt(jnp.sum(raw * raw, axis=1, keepdims=True) + epsilon_norm)
        unit[t] = raw * scale
        inverse[t] = jnp.broadcast_to(scale, (rows, 128))

    def image_start():
        yield from prepare(0)
        images[net.c, net.z] = unit[0].reshape(4, 8, width)

    def text_start():
        yield from prepare(1)
        tiles = unit[1].reshape(4, 8, width)
        texts[0, net.y, net.x] = tiles[0:2]
        texts[1, net.x, net.y] = tiles[2:4]

    def image_gather(first, length):
        def slot(z):
            return images.at[net.c, z, pl.ds(first, length)]

        def landed(relative):
            block = slot((net.z + relative + NZ) % NZ)
            across.append(net.copy(block, block, to_sib))

        yield from ring_gather(net, "z", NZ, slot, length, landed)

    def text_gather(half, first, second, counts):
        buffer = texts.at[half]
        row = buffer.at[getattr(net, second)]
        yield from ring_gather(net, first, counts[0], lambda i: row.at[i], 2)
        yield from ring_gather(net, second, counts[1], lambda i: buffer.at[i], counts[0])

    interleave([image_start(), text_start()])
    own = images.at[net.c, net.z]
    streams = [
        image_gather(0, 2),
        text_gather(0, "x", "y", (NX, NY)),
        text_gather(1, "y", "x", (NY, NX)),
        image_gather(2, 2),
    ]
    for stream in streams:
        next(stream)
    across.append(net.copy(own, own, to_sib))
    interleave(streams)
    for one in across:
        one.wait_recv()

    full = 16 * rows
    eighth = full // 8

    def split(i, carry):
        where = pl.ds(pl.multiple_of(i * eighth, eighth), eighth)
        high, low = halves(texts[i // 4, i % 4].reshape(eighth, width))
        s["text_hi"][where] = high
        s["text_lo"][where] = low
        high, low = halves(images[i // 4, pl.ds((i % 4) * 2, 2)].reshape(eighth, width))
        s["image_hi"][where] = high
        s["image_lo"][where] = low
        return carry

    lax.fori_loop(0, 8, split, 0)
    text_halves = (s["text_hi"], s["text_lo"])
    count = full // 2
    pending = {}
    for turn, c in enumerate((1 - net.c, net.c)):
        where = pl.ds(pl.multiple_of(c * count, count), count)
        image_block = (s["image_hi"][where], s["image_lo"][where])
        pair = tuple(r[...] for r in text_halves)
        logits = logit_scale * dot3(image_block, pair, ((1,), (1,))) + logit_bias
        grad_block = halves(jax.nn.sigmoid(logits) - pair_target(net, rows, c, count))
        s["image_sum"][c] = (logit_scale * dot3(grad_block, pair, ((1,), (0,)))).reshape(
            NZ, 4, 8, width
        )
        if turn == 0:
            for relative in (4, 3, -3, 2, -2, 1, -1, 0):
                z = (net.z + relative + NZ) % NZ
                pending[relative] = net.copy(
                    s["image_sum"].at[c, z], s["sibling"].at[z], to_sib
                )
        text_term = (logit_scale * dot3(grad_block, image_block, ((0,), (0,)))).reshape(
            2, NY, NX, 2, 8, width
        )
        if turn == 0:
            s["text_sum"][...] = text_term
        else:
            s["text_sum"][...] = s["text_sum"][...] + text_term

    summed = set()

    def ready(relative):
        if relative in summed:
            return
        summed.add(relative)
        z = (net.z + relative + NZ) % NZ
        pending[relative].wait_recv()
        s["sibling"][z] = s["sibling"][z] + s["image_sum"][net.c, z]

    def put(ref, *index):
        def store(value):
            ref[index] = value

        return store

    def image_reduce(k):
        where = pl.ds(2 * k, 2)
        yield from ring_reduce(
            net, "z", NZ, lambda i: s["sibling"].at[i, where], 2,
            s["z%dl" % k], s["z%dr" % k], put(s["grad"], 0, where), ready,
        )

    def text_reduce(k, first, second, counts):
        buffer, middle = s["text_sum"].at[k], s["t%dm" % k]
        yield from ring_reduce(
            net, first, counts[0], lambda i: buffer.at[i], counts[1],
            s["t%d1l" % k], s["t%d1r" % k], put(middle, ...),
        )
        yield from ring_reduce(
            net, second, counts[1], lambda i: middle.at[i], 2,
            s["t%d2l" % k], s["t%d2r" % k], put(s["grad"], 1, pl.ds(2 * k, 2)),
        )

    interleave(
        [
            text_reduce(0, "y", "x", (NY, NX)),
            text_reduce(1, "x", "y", (NX, NY)),
            image_reduce(0),
            image_reduce(1),
        ]
    )

    d_out, d_in, feature = s["d_out"], s["d_in"], s["feature"]
    exchanged = []
    for t in range(2):
        g, u = s["grad"][t].reshape(rows, width), unit[t]
        dz = inverse[t][:, :1] * (g - u * jnp.sum(u * g, axis=1, keepdims=True))
        for k in range(4):
            d_out[t, k] = dz[:, k * part : (k + 1) * part]
        exchanged.append(
            [
                net.copy(d_out.at[t, place], d_in.at[t, me], device)
                for place, device in ((far, to_far), (diag, to_diag), (sib, to_sib))
            ]
        )
        d_in[t, me] = d_out[t, me]

    lanes = width // 128
    terms, weight = s["terms"], s["weight"]

    def weight_terms(t):
        for one in exchanged[t]:
            one.wait_recv()
        dcols = halves(d_in[t].reshape(4 * rows, part))
        weight[...] = dot3(dcols, halves(group[t].reshape(4 * rows, width)), ((0,), (0,)))
        base = t * (part // 8) * lanes

        def retile(r, carry):
            strip = weight[pl.ds(pl.multiple_of(r * 8, 8), 8)]
            for j in range(lanes):
                terms[base + r * lanes + j] = strip[:, j * 128 : (j + 1) * 128]
            return carry

        lax.fori_loop(0, part // 8, retile, 0)

    def feature_stream():
        first = []
        for t in range(2):
            dcols = halves(d_in[t].reshape(4 * rows, part))
            feature[t] = dot3(dcols, halves(s["w"][t]), ((1,), (0,))).reshape(4, rows, width)
            first.append(
                (
                    net.copy(feature.at[t, diag], s["feature_in"].at[t, 0], to_sib),
                    net.copy(feature.at[t, sib], s["feature_in"].at[t, 1], to_sib),
                )
            )
        yield
        last = []
        for t in range(2):
            first[t][0].wait_recv()
            s["feature_in"][t, 0] = s["feature_in"][t, 0] + feature[t, far]
            last.append(net.copy(s["feature_in"].at[t, 0], s["feature_sum"].at[t], to_far))
        for _ in range(6):
            yield
        for t, out in ((0, image_out), (1, text_out)):
            first[t][1].wait_recv()
            last[t].wait_recv()
            out[...] = feature[t, me] + s["feature_in"][t, 1] + s["feature_sum"][t]

    def pick(prefix, *names):
        return [s[prefix + n] for n in names]

    stream_a = [
        weight_stream_a(
            net, partner, k * NZ * AZ, terms, total,
            *pick("a%d" % k, "mid", "own", "pair", "every", "zl", "zr", "yl", "yr"),
        )
        for k in range(A_STREAMS)
    ]
    stream_b = [
        weight_stream_b(
            net, partner, A_TILES + k * NY * BY, terms, total,
            *pick("b%d" % k, "mid", "own", "pair", "every", "yl", "yr", "zl", "zr"),
        )
        for k in range(B_STREAMS)
    ]
    weight_terms(0)
    for one in stream_a:
        next(one)
    weight_terms(1)
    for one in stream_b:
        next(one)
    order = [stream for pair in zip(stream_a, stream_b) for stream in pair]
    interleave([feature_stream()] + order)
    net.finish()


def pair_target(net, rows, core, count):
    i = lax.broadcasted_iota(jnp.int32, (count, 16 * rows), 0) + (core - net.c) * count
    i = i - net.z * rows
    j = lax.broadcasted_iota(jnp.int32, (count, 16 * rows), 1)
    half = rows // 2
    a = j - (net.y * NX + net.x) * half
    b = j - 8 * rows - (net.x * NY + net.y) * half + half
    same_a = (i == a) & (a >= 0) & (a < half)
    same_b = (i == b) & (b >= half) & (b < rows)
    return jnp.where(same_a | same_b, 1.0, 0.0)


def on_device(image_features, text_features, image_proj, text_proj):
    rows, width = image_features.shape
    part = image_proj.shape[1]
    shapes = scratch_shapes(rows, width, part)
    total_shape = (2 * part // 8 * (width // 128), 8, 128)
    vmem = pl.BlockSpec(memory_space=pltpu.VMEM)
    anywhere = pl.BlockSpec(memory_space=pl.ANY)
    semaphores = [pltpu.SemaphoreType.DMA((n,)) for n in (COPIES, COPIES, 2)]
    grad_image, grad_text, total = pl.pallas_call(
        functools.partial(kernel, tuple(shapes)),
        out_shape=[
            jax.ShapeDtypeStruct(shape, jnp.float32)
            for shape in ((rows, width), (rows, width), total_shape)
        ],
        in_specs=[vmem, vmem, anywhere, anywhere],
        out_specs=[vmem] * 3,
        scratch_shapes=[pltpu.VMEM(shape, kind) for shape, kind in shapes.values()] + semaphores,
        compiler_params=pltpu.CompilerParams(
            collective_id=1, has_side_effects=True, vmem_limit_bytes=60 * 2**20
        ),
    )(image_features, text_features, image_proj.T, text_proj.T)
    weights = total.reshape(2, part // 8, width // 128, 8, 128).transpose(0, 1, 3, 2, 4)
    weights = weights.reshape(2, part, width)
    return (grad_image, grad_text, weights[0].T, weights[1].T)


def solution(mesh):
    fine = Mesh(mesh.devices.reshape(NZ, NY, 2, 2, NC), ("z", "y", "xh", "xl", "core"))
    rows = P(("z", "y", "xh", "xl", "core"), None)
    cols = P(None, GROUP)
    return jax.shard_map(
        on_device,
        mesh=fine,
        in_specs=(rows, rows, cols, cols),
        out_specs=(rows, rows, cols, cols),
        check_vma=False,
    )
```

```python
import functools
import math

import jax
import jax.numpy as jnp
from jax import lax
from jax.experimental import pallas as pl
from jax.experimental.pallas import tpu as pltpu
from jax.sharding import Mesh, PartitionSpec as P

logit_scale = 100.0
logit_bias = -10.0
epsilon_norm = 1e-06
NZ, NY, NX, NC = 8, 4, 4, 2
GROUP = ("xl", "core")
MESH = pl.DeviceIdType.MESH
COPIES = 320
LINK_RATE, LINK_DELAY = 45e3, 2.0
CORE_RATE, CORE_DELAY = 350e3, 1.0


class Flight:
    def __init__(self, copy, due):
        self.copy, self.due = copy, due
        self.wait_recv, self.wait_send = copy.wait_recv, copy.wait_send


class Net:
    def __init__(self, send, recv):
        self.send, self.recv = send, recv
        self.z, self.y, self.c = (lax.axis_index(a) for a in ("z", "y", "core"))
        self.x = lax.axis_index("xh") * 2 + lax.axis_index("xl")
        self.started = []
        self.now = 0.0
        self.free = {}
        self.queue = []
        self.spawned = 0

    def device(self, z=None, y=None, x=None, c=None):
        z, y, x, c = (
            mine if other is None else other
            for mine, other in ((self.z, z), (self.y, y), (self.x, x), (self.c, c))
        )
        return (z, y, x // 2, x % 2, c)

    def along(self, axis, step):
        size = {"z": NZ, "y": NY, "x": NX, "c": NC}[axis]
        return self.device(**{axis: (getattr(self, axis) + step + size) % size})

    def copy(self, src, dst, device, link=None):
        k = len(self.started)
        one = pltpu.make_async_remote_copy(
            src_ref=src, dst_ref=dst, send_sem=self.send.at[k], recv_sem=self.recv.at[k],
            device_id=device, device_id_type=MESH,
        )
        one.start()
        size = 4.0 * math.prod(src.shape)
        if link is None:
            due = self.now + size / CORE_RATE + CORE_DELAY
        else:
            left = max(self.now, self.free.get(link, 0.0)) + size / LINK_RATE
            self.free[link] = left
            due = left + LINK_DELAY
        one = Flight(one, due)
        self.started.append(one)
        return one

    def spawn(self, stream, due=0.0):
        self.queue.append((max(self.now, due), self.spawned, stream))
        self.spawned += 1

    def barrier(self, devices):
        semaphore = pltpu.get_barrier_semaphore()
        for device in devices:
            pl.semaphore_signal(semaphore, inc=1, device_id=device, device_id_type=MESH)
        pl.semaphore_wait(semaphore, len(devices))

    def finish(self):
        assert len(self.started) <= COPIES
        for one in self.started:
            one.wait_send()


def interleave(net, streams):
    for stream in streams:
        net.spawn(stream)
    while net.queue:
        turn = min(net.queue, key=lambda entry: entry[:2])
        net.queue.remove(turn)
        due, k, stream = turn
        net.now = max(net.now, due)
        due = next(stream, None)
        if due is not None:
            net.queue.append((due, k, stream))


def ring_gather(net, axis, n, slot, length, landed=None):
    me = getattr(net, axis)
    half = n // 2
    cut = length // 2
    parts = (pl.ds(0, cut), pl.ds(cut, length - cut))
    previous = None
    for step in range(1, half + 1):
        now = []
        for way, sign in ((0, 1), (1, -1)):
            origin = slot((me - sign * (step - 1) + n) % n)
            if previous is not None:
                previous[way].wait_recv()
            if step == half:
                origin = origin.at[parts[way]]
            now.append(net.copy(origin, origin, net.along(axis, sign), (axis, sign)))
        if previous is not None and landed is not None:
            landed(step - 1)
            landed(1 - step)
        previous = now
        yield max(one.due for one in now)
    for one in previous:
        one.wait_recv()
    if landed is not None:
        landed(half)


def ring_reduce(net, axis, n, src, length, from_left, from_right, out, ready=None):
    me = getattr(net, axis)
    half = n // 2
    cut = length // 2
    parts = (pl.ds(0, cut), pl.ds(cut, length - cut))
    arrived = (from_left, from_right)
    previous = None
    for step in range(1, half + 1):
        far = half - step + 1
        now = []
        for way, sign in ((0, 1), (1, -1)):
            while ready is not None and not ready(sign * far):
                yield net.now + 0.3
            own = src((me + sign * far + n) % n)
            if step == 1:
                piece, place = own.at[parts[way]], arrived[way].at[0, parts[way]]
            else:
                previous[way].wait_recv()
                held = arrived[way].at[step - 2]
                if step == 2:
                    held[parts[way]] = held[parts[way]] + own[parts[way]]
                    held[parts[1 - way]] = own[parts[1 - way]]
                else:
                    held[...] = held[...] + own[...]
                piece, place = held, arrived[way].at[step - 1]
            now.append(net.copy(piece, place, net.along(axis, sign), (axis, sign)))
        previous = now
        yield max(one.due for one in now)
    while ready is not None and not ready(0):
        yield net.now + 0.3
    for one in previous:
        one.wait_recv()
    out(src(me)[...] + from_left[half - 1] + from_right[half - 1])


def neighbours(net):
    return [net.along(axis, step) for axis in "zyx" for step in (1, -1)]


def group_places(net):
    low, high = net.x % 2, net.x - net.x % 2
    here = (low * 2 + net.c, low * 2 + 1 - net.c)
    there = ((1 - low) * 2 + net.c, (1 - low) * 2 + 1 - net.c)
    other = high + 1 - low
    devices = (net.device(c=1 - net.c), net.device(x=other), net.device(x=other, c=1 - net.c))
    return here + there, devices


def halves(value):
    high = value.astype(jnp.bfloat16)
    return (high, (value - high.astype(jnp.float32)).astype(jnp.bfloat16))


def dot3(a, b, dims):
    def one(p, q):
        return lax.dot_general(p, q, (dims, ((), ())), preferred_element_type=jnp.float32)

    return one(a[0], b[0]) + (one(a[0], b[1]) + one(a[1], b[0]))


A_STREAMS, B_STREAMS = 2, 2
AZ, AY = 16, 2
BY, BZ = 49, 7
B_TILES = B_STREAMS * NY * BY


def weight_stream_a(net, base, part, total, mid, others, every, z0, z1):
    def store(value):
        mid[...] = value

    yield from ring_reduce(
        net, "z", NZ, lambda i: part.at[pl.ds(base + i * AZ, AZ)], AZ, z0, z1, store
    )
    high = net.x // 2
    mine = pl.ds((net.y * 2 + high) * AY, AY)
    peers = []
    for k in range(1, 2 * NY):
        y, h = (net.y + k // 2) % NY, (high + k % 2) % 2
        peers.append((pl.ds((y * 2 + h) * AY, AY), net.device(y=y, x=h * 2 + net.x % 2)))
    copies = [
        net.copy(mid.at[chunk], others.at[k], device, ("y", 1))
        for k, (chunk, device) in enumerate(peers)
    ]
    yield copies[-1].due
    for one in copies:
        one.wait_recv()
    value = mid[mine]
    for k in range(len(peers)):
        value = value + others[k]
    every[mine] = value
    copies = [
        net.copy(every.at[mine], every.at[mine], device, ("y", 1)) for _, device in peers
    ]
    yield copies[-1].due
    for one in copies:
        one.wait_recv()
    total[pl.ds(base + net.z * AZ, AZ)] = every[...]
    yield from ring_gather(net, "z", NZ, lambda i: total.at[pl.ds(base + i * AZ, AZ)], AZ)


def weight_stream_b(net, partner, base, part, total, mid, own, pair, every, y0, y1, z0, z1):
    def put(ref, index=...):
        def store(value):
            ref[index] = value

        return store

    mid[pl.ds(BY, NZ * BZ - BY)] = jnp.zeros((NZ * BZ - BY, 8, 128), jnp.float32)
    yield from ring_reduce(
        net, "y", NY, lambda i: part.at[pl.ds(base + i * BY, BY)], BY, y0, y1, put(mid, pl.ds(0, BY))
    )
    yield from ring_reduce(net, "z", NZ, lambda i: mid.at[pl.ds(i * BZ, BZ)], BZ, z0, z1, put(own))
    one = net.copy(own, pair, partner, ("x", 2))
    yield one.due + 1.0
    one.wait_recv()
    every[pl.ds(net.z * BZ, BZ)] = own[...] + pair[...]
    yield from ring_gather(net, "z", NZ, lambda i: every.at[pl.ds(i * BZ, BZ)], BZ)
    total[pl.ds(base + net.y * BY, BY)] = every[pl.ds(0, BY)]
    yield from ring_gather(net, "y", NY, lambda i: total.at[pl.ds(base + i * BY, BY)], BY)


def scratch_shapes(rows, width, part):
    tile, small = (8, width), (8, 128)
    full = 16 * rows
    f, h = jnp.float32, jnp.bfloat16
    shapes = {
        "w": ((2, part, width), f),
        "images": ((NC, NZ, 4) + tile, f),
        "texts": ((2, NY, NX, 2) + tile, f),
        "group": ((2, 4, rows, width), f),
        "unit": ((2, rows, width), f),
        "inverse": ((2, rows, 128), f),
        "col_out": ((2, 4, rows, part), f),
        "col_in": ((2, 4, rows, part), f),
        "image_hi": ((full, width), h),
        "image_lo": ((full, width), h),
        "text_hi": ((full, width), h),
        "text_lo": ((full, width), h),
        "pair_hi": ((full, full), h),
        "pair_lo": ((full, full), h),
        "image_sum": ((NC, NZ, 4) + tile, f),
        "text_sum": ((2, NY, NX, 2) + tile, f),
        "sibling": ((NZ, 4) + tile, f),
    }
    for k in range(2):
        for way in "lr":
            shapes["z%d%s" % (k, way)] = ((NZ // 2, 2) + tile, f)
    for k, (m, n) in enumerate(((NY, NX), (NX, NY))):
        shapes["t%dm" % k] = ((n, 2) + tile, f)
        for way in "lr":
            shapes["t%d1%s" % (k, way)] = ((n, m // 2, 2) + tile, f)
            shapes["t%d2%s" % (k, way)] = ((n // 2, 2) + tile, f)
    shapes["grad"] = ((2, 4) + tile, f)
    shapes["d_out"] = ((2, 4, rows, part), f)
    shapes["d_in"] = ((2, 4, rows, part), f)
    shapes["weight"] = ((part, width), f)
    shapes["terms"] = ((2 * part // 8 * (width // 128),) + small, f)
    shapes["feature"] = ((2, 4, rows, width), f)
    shapes["feature_in"] = ((2, 2, rows, width), f)
    shapes["feature_sum"] = ((2, rows, width), f)
    for k in range(A_STREAMS):
        shapes["a%dmid" % k] = ((AZ,) + small, f)
        shapes["a%dothers" % k] = ((2 * NY - 1, AY) + small, f)
        shapes["a%devery" % k] = ((AZ,) + small, f)
        for way in "lr":
            shapes["a%dz%s" % (k, way)] = ((NZ // 2, AZ) + small, f)
    for k in range(B_STREAMS):
        for name, count in zip(("mid", "own", "pair", "every"), (NZ * BZ, BZ, BZ, NZ * BZ)):
            shapes["b%d%s" % (k, name)] = ((count,) + small, f)
        for name, shape in (("y", (NY // 2, BY)), ("z", (NZ // 2, BZ))):
            for way in "lr":
                shapes["b%d%s%s" % (k, name, way)] = (shape + small, f)
    return shapes


def kernel(names, image_x, text_x, image_w, text_w, image_out, text_out, total, *scratch):
    s = dict(zip(names, scratch))
    send, recv, load = scratch[len(names) :]
    images, texts, group, unit, inverse = (
        s[n] for n in ("images", "texts", "group", "unit", "inverse")
    )
    net = Net(send, recv)
    (me, sib, far, diag), (to_sib, to_far, to_diag) = group_places(net)
    partner = net.device(x=(net.x + 2) % NX)
    rows, width = image_x.shape
    part = image_w.shape[0]

    loads = [pltpu.make_async_copy(w, s["w"].at[t], load.at[t]) for t, w in ((0, image_w), (1, text_w))]
    for one in loads:
        one.start()
    group[0, me] = image_x[...]
    group[1, me] = text_x[...]
    column = [
        net.device(y=(net.y + dy) % NY, x=(net.x + dx) % NX)
        for dy in range(NY) for dx in (0, 2) if dy == 2 or dx == 2
    ]
    net.barrier(neighbours(net) + [to_sib, to_diag] + column)

    first = []
    for t in range(2):
        block = group.at[t, me]
        first.append((net.copy(block, block, to_far, ("x", 0)), net.copy(block, block, to_sib)))
    across = []

    def prepare(t):
        loads[t].wait()
        weights = halves(s["w"][t])
        first[t][0].wait_recv()
        block = group.at[t, far]
        onward = net.copy(block, block, to_sib)
        yield onward.due
        first[t][1].wait_recv()
        onward.wait_recv()
        cols = dot3(halves(group[t].reshape(4 * rows, width)), weights, ((1,), (1,)))
        s["col_out"][t] = cols.reshape(4, rows, part)
        copies = [
            net.copy(s["col_out"].at[t, place], s["col_in"].at[t, me], device)
            for place, device in ((far, to_far), (diag, to_diag), (sib, to_sib))
        ]
        s["col_in"][t, me] = s["col_out"][t, me]
        yield copies[0].due
        for one in copies:
            one.wait_recv()
        raw = jnp.concatenate([s["col_in"][t, k] for k in range(4)], axis=1)
        scale = lax.rsqrt(jnp.sum(raw * raw, axis=1, keepdims=True) + epsilon_norm)
        unit[t] = raw * scale
        inverse[t] = jnp.broadcast_to(scale, (rows, 128))

    def image_start():
        yield from prepare(0)
        images[net.c, net.z] = unit[0].reshape(4, 8, width)
        for k in range(2):
            net.spawn(image_gather(2 * k, 2))
        own = images.at[net.c, net.z]
        across.append(net.copy(own, own, to_sib))

    def text_start():
        yield from prepare(1)
        tiles = unit[1].reshape(4, 8, width)
        texts[0, net.y, net.x] = tiles[0:2]
        texts[1, net.x, net.y] = tiles[2:4]
        net.spawn(text_gather(0, "x", "y", (NX, NY)))
        net.spawn(text_gather(1, "y", "x", (NY, NX)))

    def image_gather(first, length):
        def slot(z):
            return images.at[net.c, z, pl.ds(first, length)]

        def landed(relative):
            block = slot((net.z + relative + NZ) % NZ)
            across.append(net.copy(block, block, to_sib))

        yield from ring_gather(net, "z", NZ, slot, length, landed)

    def text_gather(half, first, second, counts):
        buffer = texts.at[half]
        row = buffer.at[getattr(net, second)]

        def landed(relative):
            i = (getattr(net, first) + relative + counts[0]) % counts[0]
            net.spawn(ring_gather(net, second, counts[1], lambda j: buffer.at[j, i], 2))

        stream = ring_gather(net, first, counts[0], lambda i: row.at[i], 2, landed)
        due = next(stream)
        landed(0)
        yield due
        yield from stream

    interleave(net, [image_start(), text_start()])
    for one in across:
        one.wait_recv()

    full = 16 * rows
    eighth = full // 8

    def split(i, carry):
        where = pl.ds(pl.multiple_of(i * eighth, eighth), eighth)
        high, low = halves(texts[i // 4, i % 4].reshape(eighth, width))
        s["text_hi"][where] = high
        s["text_lo"][where] = low
        high, low = halves(images[i // 4, pl.ds((i % 4) * 2, 2)].reshape(eighth, width))
        s["image_hi"][where] = high
        s["image_lo"][where] = low
        return carry

    lax.fori_loop(0, 8, split, 0)
    text_halves = (s["text_hi"], s["text_lo"])
    count = full // 2
    pending = {}
    for turn, c in enumerate((1 - net.c, net.c)):
        where = pl.ds(pl.multiple_of(c * count, count), count)
        image_block = (s["image_hi"][where], s["image_lo"][where])
        pair = tuple(r[...] for r in text_halves)
        logits = logit_scale * dot3(image_block, pair, ((1,), (1,))) + logit_bias
        high, low = halves(jax.nn.sigmoid(logits) - pair_target(net, rows, c, count))
        s["pair_hi"][where] = high
        s["pair_lo"][where] = low
        s["image_sum"][c] = (logit_scale * dot3((high, low), pair, ((1,), (0,)))).reshape(
            NZ, 4, 8, width
        )
        if turn == 0:
            for relative in (4, 3, -3, 2, -2, 1, -1, 0):
                z = (net.z + relative + NZ) % NZ
                pending[relative] = net.copy(
                    s["image_sum"].at[c, z], s["sibling"].at[z], to_sib
                )

    summed = set()

    def ready(relative):
        relative = relative if relative != -NZ // 2 else NZ // 2
        if relative in summed:
            return True
        summed.add(relative)
        z = (net.z + relative + NZ) % NZ
        pending[relative].wait_recv()
        s["sibling"][z] = s["sibling"][z] + s["image_sum"][net.c, z]
        return True

    def put(ref, *index):
        def store(value):
            ref[index] = value

        return store

    def image_reduce(k):
        where = pl.ds(2 * k, 2)
        yield from ring_reduce(
            net, "z", NZ, lambda i: s["sibling"].at[i, where], 2,
            s["z%dl" % k], s["z%dr" % k], put(s["grad"], 0, where), ready,
        )

    def text_reduce(k, first, second, counts):
        buffer, middle = s["text_sum"].at[k], s["t%dm" % k]
        finished = set()

        def ready(relative):
            return relative % counts[1] in finished

        def strip(relative):
            i = (getattr(net, second) + relative) % counts[1]
            yield from ring_reduce(
                net, first, counts[0], lambda j: buffer.at[j, i], 2,
                s["t%d1l" % k].at[relative], s["t%d1r" % k].at[relative], put(middle, i),
            )
            finished.add(relative)

        for relative in (2, 1, 3, 0):
            net.spawn(strip(relative))
        yield net.now + 5.0
        yield from ring_reduce(
            net, second, counts[1], lambda i: middle.at[i], 2,
            s["t%d2l" % k], s["t%d2r" % k], put(s["grad"], 1, pl.ds(2 * k, 2)), ready,
        )

    d_out, d_in, feature = s["d_out"], s["d_in"], s["feature"]

    lanes = width // 128
    terms, weight = s["terms"], s["weight"]

    def weight_terms(t):
        dcols = halves(d_in[t].reshape(4 * rows, part))
        weight[...] = dot3(dcols, halves(group[t].reshape(4 * rows, width)), ((0,), (0,)))
        base = t * (part // 8) * lanes

        def retile(r, carry):
            strip = weight[pl.ds(pl.multiple_of(r * 8, 8), 8)]
            for j in range(lanes):
                terms[base + r * lanes + j] = strip[:, j * 128 : (j + 1) * 128]
            return carry

        lax.fori_loop(0, part // 8, retile, 0)

    def feature_stream(t, out):
        dcols = halves(d_in[t].reshape(4 * rows, part))
        feature[t] = dot3(dcols, halves(s["w"][t]), ((1,), (0,))).reshape(4, rows, width)
        net.now += 1.0
        onward = net.copy(feature.at[t, diag], s["feature_in"].at[t, 0], to_sib)
        near = net.copy(feature.at[t, sib], s["feature_in"].at[t, 1], to_sib)
        yield near.due
        onward.wait_recv()
        s["feature_in"][t, 0] = s["feature_in"][t, 0] + feature[t, far]
        last = net.copy(s["feature_in"].at[t, 0], s["feature_sum"].at[t], to_far, ("x", 0))
        yield last.due + 8.0
        near.wait_recv()
        last.wait_recv()
        out[...] = feature[t, me] + s["feature_in"][t, 1] + s["feature_sum"][t]

    def pick(prefix, *names):
        return [s[prefix + n] for n in names]

    def stream_a(k):
        return weight_stream_a(
            net, B_TILES + k * NZ * AZ, terms, total,
            *pick("a%d" % k, "mid", "others", "every", "zl", "zr"),
        )

    def stream_b(k):
        return weight_stream_b(
            net, partner, k * NY * BY, terms, total,
            *pick("b%d" % k, "mid", "own", "pair", "every", "yl", "yr", "zl", "zr"),
        )

    def in_turn(streams):
        for stream in streams:
            due = next(stream)
            net.spawn(stream, due)
            yield due

    def tower(t, out, streams):
        g, u = s["grad"][t].reshape(rows, width), unit[t]
        dz = inverse[t][:, :1] * (g - u * jnp.sum(u * g, axis=1, keepdims=True))
        for k in range(4):
            d_out[t, k] = dz[:, k * part : (k + 1) * part]
        copies = [
            net.copy(d_out.at[t, place], d_in.at[t, me], device, link)
            for place, device, link in ((far, to_far, ("x", 0)), (diag, to_diag, ("x", 0)), (sib, to_sib, None))
        ]
        d_in[t, me] = d_out[t, me]
        yield copies[1].due
        for one in copies:
            one.wait_recv()
        weight_terms(t)
        net.now += 1.0
        for several in streams:
            net.spawn(in_turn(several))
        net.spawn(feature_stream(t, out), net.now + 0.5)

    unfinished = [2, 2]

    def then(t, stream, follow):
        yield from stream
        unfinished[t] -= 1
        if unfinished[t] == 0:
            net.spawn(follow)

    image_tower = tower(0, image_out, [[stream_b(k) for k in range(B_STREAMS - 1)]])
    text_tower = tower(
        1, text_out, [[stream_a(k) for k in range(A_STREAMS)], [stream_b(B_STREAMS - 1)]]
    )
    for k in range(2):
        stream = image_reduce(k)
        net.spawn(then(0, stream, image_tower), next(stream))
    image_pair = (s["image_hi"][...], s["image_lo"][...])
    grad_pair = (s["pair_hi"][...], s["pair_lo"][...])
    s["text_sum"][...] = (logit_scale * dot3(grad_pair, image_pair, ((0,), (0,)))).reshape(
        2, NY, NX, 2, 8, width
    )
    net.now += 3.0
    net.spawn(then(1, text_reduce(0, "y", "x", (NY, NX)), text_tower))
    net.spawn(then(1, text_reduce(1, "x", "y", (NX, NY)), text_tower))
    interleave(net, [])
    net.finish()


def pair_target(net, rows, core, count):
    i = lax.broadcasted_iota(jnp.int32, (count, 16 * rows), 0) + (core - net.c) * count
    i = i - net.z * rows
    j = lax.broadcasted_iota(jnp.int32, (count, 16 * rows), 1)
    half = rows // 2
    a = j - (net.y * NX + net.x) * half
    b = j - 8 * rows - (net.x * NY + net.y) * half + half
    same_a = (i == a) & (a >= 0) & (a < half)
    same_b = (i == b) & (b >= half) & (b < rows)
    return jnp.where(same_a | same_b, 1.0, 0.0)


def leave_kernel(image, text, total, image_out, text_out, first, second, semaphores):
    count = first.shape[0]
    third = count // 3
    copies = [(image, image_out), (text, text_out)]
    for t, out in ((0, first), (1, second)):
        for k in range(3):
            copies.append(
                (total.at[pl.ds(t * count + k * third, third)], out.at[pl.ds(k * third, third)])
            )
    copies = [
        pltpu.make_async_copy(src, dst, semaphores.at[k]) for k, (src, dst) in enumerate(copies)
    ]
    for one in copies:
        one.start()
    for one in copies:
        one.wait()


def on_device(image_features, text_features, image_proj, text_proj):
    rows, width = image_features.shape
    part = image_proj.shape[1]
    shapes = scratch_shapes(rows, width, part)
    total_shape = (2 * part // 8 * (width // 128), 8, 128)
    vmem = pl.BlockSpec(memory_space=pltpu.VMEM)
    anywhere = pl.BlockSpec(memory_space=pl.ANY)
    semaphores = [pltpu.SemaphoreType.DMA((n,)) for n in (COPIES, COPIES, 2)]
    grad_image, grad_text, total = pl.pallas_call(
        functools.partial(kernel, tuple(shapes)),
        out_shape=[
            jax.ShapeDtypeStruct(shape, jnp.float32)
            for shape in ((rows, width), (rows, width), total_shape)
        ],
        in_specs=[vmem, vmem, anywhere, anywhere],
        out_specs=[vmem] * 3,
        scratch_shapes=[pltpu.VMEM(shape, kind) for shape, kind in shapes.values()] + semaphores,
        compiler_params=pltpu.CompilerParams(
            collective_id=1, has_side_effects=True, vmem_limit_bytes=60 * 2**20
        ),
    )(image_features, text_features, image_proj.T, text_proj.T)
    half_shape = (part // 8 * (width // 128), 8, 128)
    grad_image, grad_text, first, second = pl.pallas_call(
        leave_kernel,
        out_shape=[
            jax.ShapeDtypeStruct(shape, jnp.float32)
            for shape in ((rows, width), (rows, width), half_shape, half_shape)
        ],
        in_specs=[vmem] * 3,
        out_specs=[anywhere] * 4,
        scratch_shapes=[pltpu.SemaphoreType.DMA((8,))],
    )(grad_image, grad_text, total)

    def untiled(tiles):
        tiles = tiles.reshape(part // 8, width // 128, 8, 128).transpose(0, 2, 1, 3)
        return tiles.reshape(part, width).T

    return (grad_image, grad_text, untiled(first), untiled(second))


def solution(mesh):
    fine = Mesh(mesh.devices.reshape(NZ, NY, 2, 2, NC), ("z", "y", "xh", "xl", "core"))
    rows = P(("z", "y", "xh", "xl", "core"), None)
    cols = P(None, GROUP)
    return jax.shard_map(
        on_device,
        mesh=fine,
        in_specs=(rows, rows, cols, cols),
        out_specs=(rows, rows, cols, cols),
        check_vma=False,
    )
```

```python
import functools
import math

import jax
import jax.numpy as jnp
from jax import lax
from jax.experimental import pallas as pl
from jax.experimental.pallas import tpu as pltpu
from jax.sharding import Mesh, PartitionSpec as P

logit_scale = 100.0
logit_bias = -10.0
epsilon_norm = 1e-06
NZ, NY, NX, NC = 8, 4, 4, 2
GROUP = ("xl", "core")
MESH = pl.DeviceIdType.MESH
COPIES = 320
LINK_RATE, LINK_DELAY = 45e3, 3.2
CORE_RATE, CORE_DELAY = 350e3, 1.0


class Flight:
    def __init__(self, copy, due):
        self.copy, self.due = copy, due
        self.wait_recv, self.wait_send = copy.wait_recv, copy.wait_send


class Net:
    def __init__(self, send, recv):
        self.send, self.recv = send, recv
        self.z, self.y, self.c = (lax.axis_index(a) for a in ("z", "y", "core"))
        self.x = lax.axis_index("xh") * 2 + lax.axis_index("xl")
        self.started = []
        self.now = 0.0
        self.free = {}
        self.queue = []
        self.spawned = 0

    def device(self, z=None, y=None, x=None, c=None):
        z, y, x, c = (
            mine if other is None else other
            for mine, other in ((self.z, z), (self.y, y), (self.x, x), (self.c, c))
        )
        return (z, y, x // 2, x % 2, c)

    def along(self, axis, step):
        size = {"z": NZ, "y": NY, "x": NX, "c": NC}[axis]
        return self.device(**{axis: (getattr(self, axis) + step + size) % size})

    def copy(self, src, dst, device, link=None):
        k = len(self.started)
        one = pltpu.make_async_remote_copy(
            src_ref=src, dst_ref=dst, send_sem=self.send.at[k], recv_sem=self.recv.at[k],
            device_id=device, device_id_type=MESH,
        )
        one.start()
        size = 4.0 * math.prod(src.shape)
        if link is None:
            due = self.now + size / CORE_RATE + CORE_DELAY
        else:
            left = max(self.now, self.free.get(link, 0.0)) + size / LINK_RATE
            self.free[link] = left
            due = left + LINK_DELAY
        one = Flight(one, due)
        self.started.append(one)
        return one

    def spawn(self, stream, due=0.0):
        self.queue.append((max(self.now, due), self.spawned, stream))
        self.spawned += 1

    def barrier(self, devices):
        semaphore = pltpu.get_barrier_semaphore()
        for device in devices:
            pl.semaphore_signal(semaphore, inc=1, device_id=device, device_id_type=MESH)
        pl.semaphore_wait(semaphore, len(devices))

    def finish(self):
        assert len(self.started) <= COPIES
        for one in self.started:
            one.wait_send()


def interleave(net, streams):
    for stream in streams:
        net.spawn(stream)
    while net.queue:
        turn = min(net.queue, key=lambda entry: entry[:2])
        net.queue.remove(turn)
        due, k, stream = turn
        net.now = max(net.now, due)
        due = next(stream, None)
        if due is not None:
            net.queue.append((due, k, stream))


def ring_gather(net, axis, n, slot, length, landed=None):
    me = getattr(net, axis)
    half = n // 2
    cut = length // 2
    parts = (pl.ds(0, cut), pl.ds(cut, length - cut))
    previous = None
    for step in range(1, half + 1):
        now = []
        for way, sign in ((0, 1), (1, -1)):
            origin = slot((me - sign * (step - 1) + n) % n)
            if previous is not None:
                previous[way].wait_recv()
            if step == half:
                origin = origin.at[parts[way]]
            now.append(net.copy(origin, origin, net.along(axis, sign), (axis, sign)))
        if previous is not None and landed is not None:
            landed(step - 1)
            landed(1 - step)
        previous = now
        yield max(one.due for one in now)
    for one in previous:
        one.wait_recv()
    if landed is not None:
        landed(half)


def ring_reduce(net, axis, n, src, length, from_left, from_right, out, ready=None):
    me = getattr(net, axis)
    half = n // 2
    cut = length // 2
    parts = (pl.ds(0, cut), pl.ds(cut, length - cut))
    arrived = (from_left, from_right)
    previous = None
    for step in range(1, half + 1):
        far = half - step + 1
        now = []
        for way, sign in ((0, 1), (1, -1)):
            while ready is not None and not ready(sign * far):
                yield net.now + 0.3
            own = src((me + sign * far + n) % n)
            if step == 1:
                piece, place = own.at[parts[way]], arrived[way].at[0, parts[way]]
            else:
                previous[way].wait_recv()
                held = arrived[way].at[step - 2]
                if step == 2:
                    held[parts[way]] = held[parts[way]] + own[parts[way]]
                    held[parts[1 - way]] = own[parts[1 - way]]
                else:
                    held[...] = held[...] + own[...]
                piece, place = held, arrived[way].at[step - 1]
            now.append(net.copy(piece, place, net.along(axis, sign), (axis, sign)))
        previous = now
        yield max(one.due for one in now)
    while ready is not None and not ready(0):
        yield net.now + 0.3
    for one in previous:
        one.wait_recv()
    out(src(me)[...] + from_left[half - 1] + from_right[half - 1])


def neighbours(net):
    return [net.along(axis, step) for axis in "zyx" for step in (1, -1)]


def group_places(net):
    low, high = net.x % 2, net.x - net.x % 2
    here = (low * 2 + net.c, low * 2 + 1 - net.c)
    there = ((1 - low) * 2 + net.c, (1 - low) * 2 + 1 - net.c)
    other = high + 1 - low
    devices = (net.device(c=1 - net.c), net.device(x=other), net.device(x=other, c=1 - net.c))
    return here + there, devices


def halves(value):
    high = value.astype(jnp.bfloat16)
    return (high, (value - high.astype(jnp.float32)).astype(jnp.bfloat16))


def dot3(a, b, dims):
    def one(p, q):
        return lax.dot_general(p, q, (dims, ((), ())), preferred_element_type=jnp.float32)

    return one(a[0], b[0]) + (one(a[0], b[1]) + one(a[1], b[0]))


A_STREAMS, B_STREAMS = 3, 2
AZ, AY = 16, 2
BY, BZ = 33, 5
B_TILES = B_STREAMS * NY * BY


def weight_stream_a(net, base, part, total, mid, others, every, z0, z1):
    def store(value):
        mid[...] = value

    yield from ring_reduce(
        net, "z", NZ, lambda i: part.at[pl.ds(base + i * AZ, AZ)], AZ, z0, z1, store
    )
    high = net.x // 2
    mine = pl.ds((net.y * 2 + high) * AY, AY)
    peers = []
    for k in range(1, 2 * NY):
        y, h = (net.y + k // 2) % NY, (high + k % 2) % 2
        peers.append((pl.ds((y * 2 + h) * AY, AY), net.device(y=y, x=h * 2 + net.x % 2)))
    copies = [
        net.copy(mid.at[chunk], others.at[k], device, ("y", 1))
        for k, (chunk, device) in enumerate(peers)
    ]
    yield copies[-1].due
    for one in copies:
        one.wait_recv()
    value = mid[mine]
    for k in range(len(peers)):
        value = value + others[k]
    every[mine] = value
    copies = [
        net.copy(every.at[mine], every.at[mine], device, ("y", 1)) for _, device in peers
    ]
    yield copies[-1].due
    for one in copies:
        one.wait_recv()
    total[pl.ds(base + net.z * AZ, AZ)] = every[...]
    yield from ring_gather(net, "z", NZ, lambda i: total.at[pl.ds(base + i * AZ, AZ)], AZ)


def weight_stream_b(net, partner, base, part, total, mid, own, pair, every, y0, y1, z0, z1):
    def put(ref, index=...):
        def store(value):
            ref[index] = value

        return store

    mid[pl.ds(BY, NZ * BZ - BY)] = jnp.zeros((NZ * BZ - BY, 8, 128), jnp.float32)
    yield from ring_reduce(
        net, "y", NY, lambda i: part.at[pl.ds(base + i * BY, BY)], BY, y0, y1, put(mid, pl.ds(0, BY))
    )
    yield from ring_reduce(net, "z", NZ, lambda i: mid.at[pl.ds(i * BZ, BZ)], BZ, z0, z1, put(own))
    one = net.copy(own, pair, partner, ("x", 2))
    yield one.due + 1.0
    one.wait_recv()
    every[pl.ds(net.z * BZ, BZ)] = own[...] + pair[...]
    yield from ring_gather(net, "z", NZ, lambda i: every.at[pl.ds(i * BZ, BZ)], BZ)
    total[pl.ds(base + net.y * BY, BY)] = every[pl.ds(0, BY)]
    yield from ring_gather(net, "y", NY, lambda i: total.at[pl.ds(base + i * BY, BY)], BY)


def scratch_shapes(rows, width, part):
    tile, small = (8, width), (8, 128)
    full = 16 * rows
    f, h = jnp.float32, jnp.bfloat16
    shapes = {
        "w": ((2, part, width), f),
        "images": ((NC, NZ, 4) + tile, f),
        "texts": ((2, NY, NX, 2) + tile, f),
        "group": ((2, 4, rows, width), f),
        "unit": ((2, rows, width), f),
        "inverse": ((2, rows, 128), f),
        "col_out": ((2, 4, rows, part), f),
        "col_in": ((2, 4, rows, part), f),
        "image_hi": ((full, width), h),
        "image_lo": ((full, width), h),
        "text_hi": ((full, width), h),
        "text_lo": ((full, width), h),
        "pair_hi": ((full, full), h),
        "pair_lo": ((full, full), h),
        "image_sum": ((NC, NZ, 4) + tile, f),
        "text_sum": ((2, NY, NX, 2) + tile, f),
        "sibling": ((NZ, 4) + tile, f),
    }
    for k in range(2):
        for way in "lr":
            shapes["z%d%s" % (k, way)] = ((NZ // 2, 2) + tile, f)
    for k, (m, n) in enumerate(((NY, NX), (NX, NY))):
        shapes["t%dm" % k] = ((n, 2) + tile, f)
        for way in "lr":
            shapes["t%d1%s" % (k, way)] = ((n, m // 2, 2) + tile, f)
            shapes["t%d2%s" % (k, way)] = ((n // 2, 2) + tile, f)
    shapes["grad"] = ((2, 4) + tile, f)
    shapes["d_out"] = ((2, 4, rows, part), f)
    shapes["d_in"] = ((2, 4, rows, part), f)
    shapes["weight"] = ((part, width), f)
    shapes["terms"] = ((2 * part // 8 * (width // 128),) + small, f)
    shapes["feature"] = ((2, 4, rows, width), f)
    shapes["feature_in"] = ((2, 2, rows, width), f)
    shapes["feature_sum"] = ((2, rows, width), f)
    for k in range(A_STREAMS):
        shapes["a%dmid" % k] = ((AZ,) + small, f)
        shapes["a%dothers" % k] = ((2 * NY - 1, AY) + small, f)
        shapes["a%devery" % k] = ((AZ,) + small, f)
        for way in "lr":
            shapes["a%dz%s" % (k, way)] = ((NZ // 2, AZ) + small, f)
    for k in range(B_STREAMS):
        for name, count in zip(("mid", "own", "pair", "every"), (NZ * BZ, BZ, BZ, NZ * BZ)):
            shapes["b%d%s" % (k, name)] = ((count,) + small, f)
        for name, shape in (("y", (NY // 2, BY)), ("z", (NZ // 2, BZ))):
            for way in "lr":
                shapes["b%d%s%s" % (k, name, way)] = (shape + small, f)
    return shapes


def kernel(names, image_x, text_x, image_w, text_w, image_out, text_out, total, *scratch):
    s = dict(zip(names, scratch))
    send, recv, load = scratch[len(names) :]
    images, texts, group, unit, inverse = (
        s[n] for n in ("images", "texts", "group", "unit", "inverse")
    )
    net = Net(send, recv)
    (me, sib, far, diag), (to_sib, to_far, to_diag) = group_places(net)
    rows, width = image_x.shape
    part = image_w.shape[0]

    loads = [pltpu.make_async_copy(w, s["w"].at[t], load.at[t]) for t, w in ((0, image_w), (1, text_w))]
    for one in loads:
        one.start()
    group[0, me] = image_x[...]
    group[1, me] = text_x[...]
    column = [
        net.device(y=(net.y + dy) % NY, x=(net.x + dx) % NX)
        for dy in range(NY) for dx in (0, 2) if dy == 2 or dx == 2
    ]
    net.barrier(neighbours(net) + [to_sib, to_diag] + column)

    first = []
    for t in range(2):
        block = group.at[t, me]
        first.append((net.copy(block, block, to_far, ("x", 0)), net.copy(block, block, to_sib)))
    across = []

    def prepare(t):
        loads[t].wait()
        weights = halves(s["w"][t])
        first[t][0].wait_recv()
        block = group.at[t, far]
        onward = net.copy(block, block, to_sib)
        yield onward.due
        first[t][1].wait_recv()
        onward.wait_recv()
        cols = dot3(halves(group[t].reshape(4 * rows, width)), weights, ((1,), (1,)))
        s["col_out"][t] = cols.reshape(4, rows, part)
        copies = [
            net.copy(s["col_out"].at[t, place], s["col_in"].at[t, me], device)
            for place, device in ((far, to_far), (diag, to_diag), (sib, to_sib))
        ]
        s["col_in"][t, me] = s["col_out"][t, me]
        yield copies[0].due
        for one in copies:
            one.wait_recv()
        raw = jnp.concatenate([s["col_in"][t, k] for k in range(4)], axis=1)
        scale = lax.rsqrt(jnp.sum(raw * raw, axis=1, keepdims=True) + epsilon_norm)
        unit[t] = raw * scale
        inverse[t] = jnp.broadcast_to(scale, (rows, 128))

    def image_start():
        yield from prepare(0)
        images[net.c, net.z] = unit[0].reshape(4, 8, width)
        for k in range(2):
            net.spawn(image_gather(2 * k, 2))
        own = images.at[net.c, net.z]
        across.append(net.copy(own, own, to_sib))

    def text_start():
        yield from prepare(1)
        tiles = unit[1].reshape(4, 8, width)
        texts[0, net.y, net.x] = tiles[0:2]
        texts[1, net.x, net.y] = tiles[2:4]
        net.spawn(text_gather(0, "x", "y", (NX, NY)))
        net.spawn(text_gather(1, "y", "x", (NY, NX)))

    def image_gather(first, length):
        def slot(z):
            return images.at[net.c, z, pl.ds(first, length)]

        def landed(relative):
            block = slot((net.z + relative + NZ) % NZ)
            across.append(net.copy(block, block, to_sib))

        yield from ring_gather(net, "z", NZ, slot, length, landed)

    def text_gather(half, first, second, counts):
        buffer = texts.at[half]
        row = buffer.at[getattr(net, second)]

        def landed(relative):
            i = (getattr(net, first) + relative + counts[0]) % counts[0]
            net.spawn(ring_gather(net, second, counts[1], lambda j: buffer.at[j, i], 2))

        stream = ring_gather(net, first, counts[0], lambda i: row.at[i], 2, landed)
        due = next(stream)
        landed(0)
        yield due
        yield from stream

    interleave(net, [image_start(), text_start()])
    for one in across:
        one.wait_recv()

    full = 16 * rows
    eighth = full // 8

    def split(i, carry):
        where = pl.ds(pl.multiple_of(i * eighth, eighth), eighth)
        high, low = halves(texts[i // 4, i % 4].reshape(eighth, width))
        s["text_hi"][where] = high
        s["text_lo"][where] = low
        high, low = halves(images[i // 4, pl.ds((i % 4) * 2, 2)].reshape(eighth, width))
        s["image_hi"][where] = high
        s["image_lo"][where] = low
        return carry

    lax.fori_loop(0, 8, split, 0)
    text_halves = (s["text_hi"], s["text_lo"])
    count = full // 2
    pending = {}
    for turn, c in enumerate((1 - net.c, net.c)):
        where = pl.ds(pl.multiple_of(c * count, count), count)
        image_block = (s["image_hi"][where], s["image_lo"][where])
        pair = tuple(r[...] for r in text_halves)
        logits = logit_scale * dot3(image_block, pair, ((1,), (1,))) + logit_bias
        high, low = halves(jax.nn.sigmoid(logits) - pair_target(net, rows, c, count))
        s["pair_hi"][where] = high
        s["pair_lo"][where] = low
        s["image_sum"][c] = (logit_scale * dot3((high, low), pair, ((1,), (0,)))).reshape(
            NZ, 4, 8, width
        )
        if turn == 0:
            for relative in (4, 3, -3, 2, -2, 1, -1, 0):
                z = (net.z + relative + NZ) % NZ
                pending[relative] = net.copy(
                    s["image_sum"].at[c, z], s["sibling"].at[z], to_sib
                )

    summed = set()

    def ready(relative):
        relative = relative if relative != -NZ // 2 else NZ // 2
        if relative in summed:
            return True
        summed.add(relative)
        z = (net.z + relative + NZ) % NZ
        pending[relative].wait_recv()
        s["sibling"][z] = s["sibling"][z] + s["image_sum"][net.c, z]
        return True

    def put(ref, *index):
        def store(value):
            ref[index] = value

        return store

    def image_reduce(k):
        where = pl.ds(2 * k, 2)
        yield from ring_reduce(
            net, "z", NZ, lambda i: s["sibling"].at[i, where], 2,
            s["z%dl" % k], s["z%dr" % k], put(s["grad"], 0, where), ready,
        )

    def text_reduce(k, first, second, counts):
        buffer, middle = s["text_sum"].at[k], s["t%dm" % k]
        finished = set()

        def ready(relative):
            return relative % counts[1] in finished

        def strip(relative):
            i = (getattr(net, second) + relative) % counts[1]
            yield from ring_reduce(
                net, first, counts[0], lambda j: buffer.at[j, i], 2,
                s["t%d1l" % k].at[relative], s["t%d1r" % k].at[relative], put(middle, i),
            )
            finished.add(relative)

        for relative in (2, 1, 3, 0):
            net.spawn(strip(relative))
        yield net.now + 5.0
        yield from ring_reduce(
            net, second, counts[1], lambda i: middle.at[i], 2,
            s["t%d2l" % k], s["t%d2r" % k], put(s["grad"], 1, pl.ds(2 * k, 2)), ready,
        )

    d_out, d_in, feature = s["d_out"], s["d_in"], s["feature"]

    lanes = width // 128
    terms, weight = s["terms"], s["weight"]

    def weight_terms(t):
        dcols = halves(d_in[t].reshape(4 * rows, part))
        weight[...] = dot3(dcols, halves(group[t].reshape(4 * rows, width)), ((0,), (0,)))
        base = t * (part // 8) * lanes

        def retile(r, carry):
            strip = weight[pl.ds(pl.multiple_of(r * 8, 8), 8)]
            for j in range(lanes):
                terms[base + r * lanes + j] = strip[:, j * 128 : (j + 1) * 128]
            return carry

        lax.fori_loop(0, part // 8, retile, 0)

    def feature_stream(t, out):
        dcols = halves(d_in[t].reshape(4 * rows, part))
        feature[t] = dot3(dcols, halves(s["w"][t]), ((1,), (0,))).reshape(4, rows, width)
        net.now += 1.0
        onward = net.copy(feature.at[t, diag], s["feature_in"].at[t, 0], to_sib)
        near = net.copy(feature.at[t, sib], s["feature_in"].at[t, 1], to_sib)
        yield near.due
        onward.wait_recv()
        s["feature_in"][t, 0] = s["feature_in"][t, 0] + feature[t, far]
        last = net.copy(s["feature_in"].at[t, 0], s["feature_sum"].at[t], to_far, ("x", 0))
        yield last.due + 8.0
        near.wait_recv()
        last.wait_recv()
        out[...] = feature[t, me] + s["feature_in"][t, 1] + s["feature_sum"][t]

    def pick(prefix, *names):
        return [s[prefix + n] for n in names]

    def stream_a(k):
        return weight_stream_a(
            net, B_TILES + k * NZ * AZ, terms, total,
            *pick("a%d" % k, "mid", "others", "every", "zl", "zr"),
        )

    def stream_b(k):
        return weight_stream_b(
            net, net.device(x=(net.x + 2) % NX), k * NY * BY, terms, total,
            *pick("b%d" % k, "mid", "own", "pair", "every", "yl", "yr", "zl", "zr"),
        )

    def in_turn(streams):
        for stream in streams:
            due = next(stream)
            net.spawn(stream, due)
            yield due

    def tower(t, out, streams):
        g, u = s["grad"][t].reshape(rows, width), unit[t]
        dz = inverse[t][:, :1] * (g - u * jnp.sum(u * g, axis=1, keepdims=True))
        for k in range(4):
            d_out[t, k] = dz[:, k * part : (k + 1) * part]
        copies = [
            net.copy(d_out.at[t, place], d_in.at[t, me], device, link)
            for place, device, link in ((far, to_far, ("x", 0)), (diag, to_diag, ("x", 0)), (sib, to_sib, None))
        ]
        d_in[t, me] = d_out[t, me]
        yield copies[1].due
        for one in copies:
            one.wait_recv()
        weight_terms(t)
        net.now += 1.0
        for several in streams:
            net.spawn(in_turn(several))
        net.spawn(feature_stream(t, out), net.now + 0.5)

    unfinished = [2, 2]

    def then(t, stream, follow):
        yield from stream
        unfinished[t] -= 1
        if unfinished[t] == 0:
            net.spawn(follow)

    image_tower = tower(0, image_out, [[stream_b(k) for k in range(B_STREAMS)]])
    text_tower = tower(
        1, text_out, [[stream_a(k) for k in range(A_STREAMS)]]
    )
    for k in range(2):
        stream = image_reduce(k)
        net.spawn(then(0, stream, image_tower), next(stream))
    image_pair = (s["image_hi"][...], s["image_lo"][...])
    grad_pair = (s["pair_hi"][...], s["pair_lo"][...])
    s["text_sum"][...] = (logit_scale * dot3(grad_pair, image_pair, ((0,), (0,)))).reshape(
        2, NY, NX, 2, 8, width
    )
    net.now += 3.0
    net.spawn(then(1, text_reduce(0, "y", "x", (NY, NX)), text_tower))
    net.spawn(then(1, text_reduce(1, "x", "y", (NX, NY)), text_tower))
    interleave(net, [])
    net.finish()


def pair_target(net, rows, core, count):
    i = lax.broadcasted_iota(jnp.int32, (count, 16 * rows), 0) + (core - net.c) * count
    i = i - net.z * rows
    j = lax.broadcasted_iota(jnp.int32, (count, 16 * rows), 1)
    half = rows // 2
    a = j - (net.y * NX + net.x) * half
    b = j - 8 * rows - (net.x * NY + net.y) * half + half
    same_a = (i == a) & (a >= 0) & (a < half)
    same_b = (i == b) & (b >= half) & (b < rows)
    return jnp.where(same_a | same_b, 1.0, 0.0)


def leave_kernel(image, text, total, image_out, text_out, first, second,
                 image_held, text_held, held, arrived, left):
    count = first.shape[0]
    third = count // 3
    moves = []
    for t, out in ((0, first), (1, second)):
        for k in range(3):
            there, here = pl.ds(t * count + k * third, third), pl.ds(k * third, third)
            moves.append((total.at[there], held.at[there], out.at[here]))
    moves += [(image, image_held, image_out), (text, text_held, text_out)]
    reads = [
        pltpu.make_async_copy(src, mid, arrived.at[k]) for k, (src, mid, _) in enumerate(moves)
    ]
    writes = [pltpu.make_async_copy(mid, out, left.at[k]) for k, (_, mid, out) in enumerate(moves)]
    for one in reads:
        one.start()
    for read, write in zip(reads, writes):
        read.wait()
        write.start()
    for one in writes:
        one.wait()


def on_device(image_features, text_features, image_proj, text_proj):
    rows, width = image_features.shape
    part = image_proj.shape[1]
    shapes = scratch_shapes(rows, width, part)
    total_shape = (2 * part // 8 * (width // 128), 8, 128)
    vmem = pl.BlockSpec(memory_space=pltpu.VMEM)
    anywhere = pl.BlockSpec(memory_space=pl.ANY)
    hbm = pl.BlockSpec(memory_space=pltpu.HBM)
    semaphores = [pltpu.SemaphoreType.DMA((n,)) for n in (COPIES, COPIES, 2)]
    grad_image, grad_text, total = pl.pallas_call(
        functools.partial(kernel, tuple(shapes)),
        out_shape=[
            jax.ShapeDtypeStruct(shape, jnp.float32)
            for shape in ((rows, width), (rows, width), total_shape)
        ],
        in_specs=[vmem, vmem, anywhere, anywhere],
        out_specs=[vmem] * 3,
        scratch_shapes=[pltpu.VMEM(shape, kind) for shape, kind in shapes.values()] + semaphores,
        compiler_params=pltpu.CompilerParams(
            collective_id=1, has_side_effects=True, vmem_limit_bytes=60 * 2**20
        ),
    )(image_features, text_features, image_proj.T, text_proj.T)
    half_shape = (part // 8 * (width // 128), 8, 128)
    grad_image, grad_text, first, second = pl.pallas_call(
        leave_kernel,
        out_shape=[
            jax.ShapeDtypeStruct(shape, jnp.float32)
            for shape in ((rows, width), (rows, width), half_shape, half_shape)
        ],
        in_specs=[hbm] * 3,
        out_specs=[hbm] * 4,
        scratch_shapes=[
            pltpu.VMEM(shape, jnp.float32) for shape in ((rows, width), (rows, width), total_shape)
        ]
        + [pltpu.SemaphoreType.DMA((8,))] * 2,
    )(grad_image, grad_text, total)

    def untiled(tiles):
        tiles = tiles.reshape(part // 8, width // 128, 8, 128).transpose(0, 2, 1, 3)
        return tiles.reshape(part, width).T

    return (grad_image, grad_text, untiled(first), untiled(second))


def solution(mesh):
    fine = Mesh(mesh.devices.reshape(NZ, NY, 2, 2, NC), ("z", "y", "xh", "xl", "core"))
    rows = P(("z", "y", "xh", "xl", "core"), None)
    cols = P(None, GROUP)
    return jax.shard_map(
        on_device,
        mesh=fine,
        in_specs=(rows, rows, cols, cols),
        out_specs=(rows, rows, cols, cols),
        check_vma=False,
    )
```

```python
import functools
import math

import jax
import jax.numpy as jnp
from jax import lax
from jax.experimental import pallas as pl
from jax.experimental.pallas import tpu as pltpu
from jax.sharding import Mesh, PartitionSpec as P

logit_scale = 100.0
logit_bias = -10.0
epsilon_norm = 1e-06
NZ, NY, NX, NC = 8, 4, 4, 2
GROUP = ("xl", "core")
MESH = pl.DeviceIdType.MESH
COPIES = 320
LINK_RATE, LINK_DELAY = 45e3, 3.2
CORE_RATE, CORE_DELAY = 350e3, 1.0


class Flight:
    def __init__(self, copy, due):
        self.copy, self.due = copy, due
        self.wait_recv, self.wait_send = copy.wait_recv, copy.wait_send


class Net:
    def __init__(self, send, recv):
        self.send, self.recv = send, recv
        self.z, self.y, self.c = (lax.axis_index(a) for a in ("z", "y", "core"))
        self.x = lax.axis_index("xh") * 2 + lax.axis_index("xl")
        self.started = []
        self.now = 0.0
        self.free = {}
        self.queue = []
        self.spawned = 0

    def device(self, z=None, y=None, x=None, c=None):
        z, y, x, c = (
            mine if other is None else other
            for mine, other in ((self.z, z), (self.y, y), (self.x, x), (self.c, c))
        )
        return (z, y, x // 2, x % 2, c)

    def along(self, axis, step):
        size = {"z": NZ, "y": NY, "x": NX, "c": NC}[axis]
        return self.device(**{axis: (getattr(self, axis) + step + size) % size})

    def copy(self, src, dst, device, link=None):
        k = len(self.started)
        one = pltpu.make_async_remote_copy(
            src_ref=src, dst_ref=dst, send_sem=self.send.at[k], recv_sem=self.recv.at[k],
            device_id=device, device_id_type=MESH,
        )
        one.start()
        size = 4.0 * math.prod(src.shape)
        if link is None:
            due = self.now + size / CORE_RATE + CORE_DELAY
        else:
            left = max(self.now, self.free.get(link, 0.0)) + size / LINK_RATE
            self.free[link] = left
            due = left + LINK_DELAY
        one = Flight(one, due)
        self.started.append(one)
        return one

    def spawn(self, stream, due=0.0):
        self.queue.append((max(self.now, due), self.spawned, stream))
        self.spawned += 1

    def barrier(self, devices):
        semaphore = pltpu.get_barrier_semaphore()
        for device in devices:
            pl.semaphore_signal(semaphore, inc=1, device_id=device, device_id_type=MESH)
        pl.semaphore_wait(semaphore, len(devices))

    def finish(self):
        assert len(self.started) <= COPIES
        for one in self.started:
            one.wait_send()


def interleave(net, streams):
    for stream in streams:
        net.spawn(stream)
    while net.queue:
        turn = min(net.queue, key=lambda entry: entry[:2])
        net.queue.remove(turn)
        due, k, stream = turn
        net.now = max(net.now, due)
        due = next(stream, None)
        if due is not None:
            net.queue.append((due, k, stream))


def ring_gather(net, axis, n, slot, length, landed=None):
    me = getattr(net, axis)
    half = n // 2
    cut = length // 2
    parts = (pl.ds(0, cut), pl.ds(cut, length - cut))
    previous = None
    for step in range(1, half + 1):
        now = []
        for way, sign in ((0, 1), (1, -1)):
            origin = slot((me - sign * (step - 1) + n) % n)
            if previous is not None:
                previous[way].wait_recv()
            if step == half:
                origin = origin.at[parts[way]]
            now.append(net.copy(origin, origin, net.along(axis, sign), (axis, sign)))
        if previous is not None and landed is not None:
            landed(step - 1)
            landed(1 - step)
        previous = now
        yield max(one.due for one in now)
    for one in previous:
        one.wait_recv()
    if landed is not None:
        landed(half)


def ring_reduce(net, axis, n, src, length, from_left, from_right, out, ready=None):
    me = getattr(net, axis)
    half = n // 2
    cut = length // 2
    parts = (pl.ds(0, cut), pl.ds(cut, length - cut))
    arrived = (from_left, from_right)
    previous = None
    for step in range(1, half + 1):
        far = half - step + 1
        now = []
        for way, sign in ((0, 1), (1, -1)):
            while ready is not None and not ready(sign * far):
                yield net.now + 0.3
            own = src((me + sign * far + n) % n)
            if step == 1:
                piece, place = own.at[parts[way]], arrived[way].at[0, parts[way]]
            else:
                previous[way].wait_recv()
                held = arrived[way].at[step - 2]
                if step == 2:
                    held[parts[way]] = held[parts[way]] + own[parts[way]]
                    held[parts[1 - way]] = own[parts[1 - way]]
                else:
                    held[...] = held[...] + own[...]
                piece, place = held, arrived[way].at[step - 1]
            now.append(net.copy(piece, place, net.along(axis, sign), (axis, sign)))
        previous = now
        yield max(one.due for one in now)
    while ready is not None and not ready(0):
        yield net.now + 0.3
    for one in previous:
        one.wait_recv()
    out(src(me)[...] + from_left[half - 1] + from_right[half - 1])


def neighbours(net):
    return [net.along(axis, step) for axis in "zyx" for step in (1, -1)]


def group_places(net):
    low, high = net.x % 2, net.x - net.x % 2
    here = (low * 2 + net.c, low * 2 + 1 - net.c)
    there = ((1 - low) * 2 + net.c, (1 - low) * 2 + 1 - net.c)
    other = high + 1 - low
    devices = (net.device(c=1 - net.c), net.device(x=other), net.device(x=other, c=1 - net.c))
    return here + there, devices


def halves(value):
    high = value.astype(jnp.bfloat16)
    return (high, (value - high.astype(jnp.float32)).astype(jnp.bfloat16))


def dot3(a, b, dims):
    def one(p, q):
        return lax.dot_general(p, q, (dims, ((), ())), preferred_element_type=jnp.float32)

    return one(a[0], b[0]) + (one(a[0], b[1]) + one(a[1], b[0]))


A_STREAMS, B_STREAMS = 3, 2
AZ, AY = 16, 2
BY, BZ = 33, 5
B_TILES = B_STREAMS * NY * BY


def weight_stream_a(net, base, part, total, mid, others, every, z0, z1):
    def store(value):
        mid[...] = value

    yield from ring_reduce(
        net, "z", NZ, lambda i: part.at[pl.ds(base + i * AZ, AZ)], AZ, z0, z1, store
    )
    high = net.x // 2
    mine = pl.ds((net.y * 2 + high) * AY, AY)
    peers = []
    for k in range(1, 2 * NY):
        y, h = (net.y + k // 2) % NY, (high + k % 2) % 2
        peers.append((pl.ds((y * 2 + h) * AY, AY), net.device(y=y, x=h * 2 + net.x % 2)))
    copies = [
        net.copy(mid.at[chunk], others.at[k], device, ("y", 1))
        for k, (chunk, device) in enumerate(peers)
    ]
    yield copies[-1].due
    for one in copies:
        one.wait_recv()
    value = mid[mine]
    for k in range(len(peers)):
        value = value + others[k]
    every[mine] = value
    copies = [
        net.copy(every.at[mine], every.at[mine], device, ("y", 1)) for _, device in peers
    ]
    yield copies[-1].due
    for one in copies:
        one.wait_recv()
    total[pl.ds(base + net.z * AZ, AZ)] = every[...]
    yield from ring_gather(net, "z", NZ, lambda i: total.at[pl.ds(base + i * AZ, AZ)], AZ)


def weight_stream_b(net, partner, base, part, total, mid, own, pair, every, y0, y1, z0, z1):
    def put(ref, index=...):
        def store(value):
            ref[index] = value

        return store

    mid[pl.ds(BY, NZ * BZ - BY)] = jnp.zeros((NZ * BZ - BY, 8, 128), jnp.float32)
    yield from ring_reduce(
        net, "y", NY, lambda i: part.at[pl.ds(base + i * BY, BY)], BY, y0, y1, put(mid, pl.ds(0, BY))
    )
    yield from ring_reduce(net, "z", NZ, lambda i: mid.at[pl.ds(i * BZ, BZ)], BZ, z0, z1, put(own))
    one = net.copy(own, pair, partner, ("x", 2))
    yield one.due + 1.0
    one.wait_recv()
    every[pl.ds(net.z * BZ, BZ)] = own[...] + pair[...]
    yield from ring_gather(net, "z", NZ, lambda i: every.at[pl.ds(i * BZ, BZ)], BZ)
    total[pl.ds(base + net.y * BY, BY)] = every[pl.ds(0, BY)]
    yield from ring_gather(net, "y", NY, lambda i: total.at[pl.ds(base + i * BY, BY)], BY)


def scratch_shapes(rows, width, part):
    tile, small = (8, width), (8, 128)
    full = 16 * rows
    f, h = jnp.float32, jnp.bfloat16
    shapes = {
        "w": ((2, part, width), f),
        "images": ((NC, NZ, 4) + tile, f),
        "texts": ((2, NY, NX, 2) + tile, f),
        "group": ((2, 4, rows, width), f),
        "unit": ((2, rows, width), f),
        "inverse": ((2, rows, 128), f),
        "col_out": ((2, 4, rows, part), f),
        "col_in": ((2, 4, rows, part), f),
        "image_hi": ((full, width), h),
        "image_lo": ((full, width), h),
        "text_hi": ((full, width), h),
        "text_lo": ((full, width), h),
        "pair_hi": ((full, full), h),
        "pair_lo": ((full, full), h),
        "image_sum": ((NC, NZ, 4) + tile, f),
        "text_sum": ((2, NY, NX, 2) + tile, f),
        "sibling": ((NZ, 4) + tile, f),
    }
    for k in range(2):
        for way in "lr":
            shapes["z%d%s" % (k, way)] = ((NZ // 2, 2) + tile, f)
    for k, (m, n) in enumerate(((NY, NX), (NX, NY))):
        shapes["t%dm" % k] = ((n, 2) + tile, f)
        for way in "lr":
            shapes["t%d1%s" % (k, way)] = ((n, m // 2, 2) + tile, f)
            shapes["t%d2%s" % (k, way)] = ((n // 2, 2) + tile, f)
    shapes["grad"] = ((2, 4) + tile, f)
    shapes["d_out"] = ((2, 4, rows, part), f)
    shapes["d_in"] = ((2, 4, rows, part), f)
    shapes["weight"] = ((part, width), f)
    shapes["terms"] = ((2 * part // 8 * (width // 128),) + small, f)
    shapes["feature"] = ((2, 4, rows, width), f)
    shapes["feature_in"] = ((2, 2, rows, width), f)
    shapes["feature_sum"] = ((2, rows, width), f)
    for k in range(A_STREAMS):
        shapes["a%dmid" % k] = ((AZ,) + small, f)
        shapes["a%dothers" % k] = ((2 * NY - 1, AY) + small, f)
        shapes["a%devery" % k] = ((AZ,) + small, f)
        for way in "lr":
            shapes["a%dz%s" % (k, way)] = ((NZ // 2, AZ) + small, f)
    for k in range(B_STREAMS):
        for name, count in zip(("mid", "own", "pair", "every"), (NZ * BZ, BZ, BZ, NZ * BZ)):
            shapes["b%d%s" % (k, name)] = ((count,) + small, f)
        for name, shape in (("y", (NY // 2, BY)), ("z", (NZ // 2, BZ))):
            for way in "lr":
                shapes["b%d%s%s" % (k, name, way)] = (shape + small, f)
    return shapes


def kernel(names, image_x, text_x, image_w, text_w, image_out, text_out, total, *scratch):
    s = dict(zip(names, scratch))
    send, recv, load = scratch[len(names) :]
    images, texts, group, unit, inverse = (
        s[n] for n in ("images", "texts", "group", "unit", "inverse")
    )
    net = Net(send, recv)
    (me, sib, far, diag), (to_sib, to_far, to_diag) = group_places(net)
    rows, width = image_x.shape
    part = image_w.shape[0]

    loads = [pltpu.make_async_copy(w, s["w"].at[t], load.at[t]) for t, w in ((0, image_w), (1, text_w))]
    for one in loads:
        one.start()
    group[0, me] = image_x[...]
    group[1, me] = text_x[...]
    column = [
        net.device(y=(net.y + dy) % NY, x=(net.x + dx) % NX)
        for dy in range(NY) for dx in (0, 2) if dy == 2 or dx == 2
    ]
    net.barrier(neighbours(net) + [to_sib, to_diag] + column)

    first = []
    for t in range(2):
        block = group.at[t, me]
        first.append((net.copy(block, block, to_far, ("x", 0)), net.copy(block, block, to_sib)))
    across = []

    def prepare(t):
        loads[t].wait()
        weights = halves(s["w"][t])
        first[t][0].wait_recv()
        block = group.at[t, far]
        onward = net.copy(block, block, to_sib)
        yield onward.due
        first[t][1].wait_recv()
        onward.wait_recv()
        cols = dot3(halves(group[t].reshape(4 * rows, width)), weights, ((1,), (1,)))
        s["col_out"][t] = cols.reshape(4, rows, part)
        copies = [
            net.copy(s["col_out"].at[t, place], s["col_in"].at[t, me], device)
            for place, device in ((far, to_far), (diag, to_diag), (sib, to_sib))
        ]
        s["col_in"][t, me] = s["col_out"][t, me]
        yield copies[0].due
        for one in copies:
            one.wait_recv()
        raw = jnp.concatenate([s["col_in"][t, k] for k in range(4)], axis=1)
        scale = lax.rsqrt(jnp.sum(raw * raw, axis=1, keepdims=True) + epsilon_norm)
        unit[t] = raw * scale
        inverse[t] = jnp.broadcast_to(scale, (rows, 128))

    def image_start():
        yield from prepare(0)
        images[net.c, net.z] = unit[0].reshape(4, 8, width)
        for k in range(2):
            net.spawn(image_gather(2 * k, 2))
        own = images.at[net.c, net.z]
        across.append(net.copy(own, own, to_sib))

    def text_start():
        yield from prepare(1)
        tiles = unit[1].reshape(4, 8, width)
        texts[0, net.y, net.x] = tiles[0:2]
        texts[1, net.x, net.y] = tiles[2:4]
        net.spawn(text_gather(0, "x", "y", (NX, NY)))
        net.spawn(text_gather(1, "y", "x", (NY, NX)))

    def image_gather(first, length):
        def slot(z):
            return images.at[net.c, z, pl.ds(first, length)]

        def landed(relative):
            block = slot((net.z + relative + NZ) % NZ)
            across.append(net.copy(block, block, to_sib))

        yield from ring_gather(net, "z", NZ, slot, length, landed)

    def text_gather(half, first, second, counts):
        buffer = texts.at[half]
        row = buffer.at[getattr(net, second)]

        def landed(relative):
            i = (getattr(net, first) + relative + counts[0]) % counts[0]
            net.spawn(ring_gather(net, second, counts[1], lambda j: buffer.at[j, i], 2))

        stream = ring_gather(net, first, counts[0], lambda i: row.at[i], 2, landed)
        due = next(stream)
        landed(0)
        yield due
        yield from stream

    interleave(net, [image_start(), text_start()])
    for one in across:
        one.wait_recv()

    full = 16 * rows
    eighth = full // 8

    def split(i, carry):
        where = pl.ds(pl.multiple_of(i * eighth, eighth), eighth)
        high, low = halves(texts[i // 4, i % 4].reshape(eighth, width))
        s["text_hi"][where] = high
        s["text_lo"][where] = low
        high, low = halves(images[i // 4, pl.ds((i % 4) * 2, 2)].reshape(eighth, width))
        s["image_hi"][where] = high
        s["image_lo"][where] = low
        return carry

    lax.fori_loop(0, 8, split, 0)
    text_halves = (s["text_hi"], s["text_lo"])
    count = full // 2
    pending = {}
    for turn, c in enumerate((1 - net.c, net.c)):
        where = pl.ds(pl.multiple_of(c * count, count), count)
        image_block = (s["image_hi"][where], s["image_lo"][where])
        pair = tuple(r[...] for r in text_halves)
        logits = logit_scale * dot3(image_block, pair, ((1,), (1,))) + logit_bias
        high, low = halves(jax.nn.sigmoid(logits) - pair_target(net, rows, c, count))
        s["pair_hi"][where] = high
        s["pair_lo"][where] = low
        s["image_sum"][c] = (logit_scale * dot3((high, low), pair, ((1,), (0,)))).reshape(
            NZ, 4, 8, width
        )
        if turn == 0:
            for relative in (4, 3, -3, 2, -2, 1, -1, 0):
                z = (net.z + relative + NZ) % NZ
                pending[relative] = net.copy(
                    s["image_sum"].at[c, z], s["sibling"].at[z], to_sib
                )

    summed = set()

    def ready(relative):
        relative = relative if relative != -NZ // 2 else NZ // 2
        if relative in summed:
            return True
        summed.add(relative)
        z = (net.z + relative + NZ) % NZ
        pending[relative].wait_recv()
        s["sibling"][z] = s["sibling"][z] + s["image_sum"][net.c, z]
        return True

    def put(ref, *index):
        def store(value):
            ref[index] = value

        return store

    def image_reduce(k):
        where = pl.ds(2 * k, 2)
        yield from ring_reduce(
            net, "z", NZ, lambda i: s["sibling"].at[i, where], 2,
            s["z%dl" % k], s["z%dr" % k], put(s["grad"], 0, where), ready,
        )

    def text_reduce(k, first, second, counts):
        buffer, middle = s["text_sum"].at[k], s["t%dm" % k]
        finished = set()

        def ready(relative):
            return relative % counts[1] in finished

        def strip(relative):
            i = (getattr(net, second) + relative) % counts[1]
            yield from ring_reduce(
                net, first, counts[0], lambda j: buffer.at[j, i], 2,
                s["t%d1l" % k].at[relative], s["t%d1r" % k].at[relative], put(middle, i),
            )
            finished.add(relative)

        for relative in (2, 1, 3, 0):
            net.spawn(strip(relative))
        yield net.now + 5.0
        yield from ring_reduce(
            net, second, counts[1], lambda i: middle.at[i], 2,
            s["t%d2l" % k], s["t%d2r" % k], put(s["grad"], 1, pl.ds(2 * k, 2)), ready,
        )

    d_out, d_in, feature = s["d_out"], s["d_in"], s["feature"]

    lanes = width // 128
    terms, weight = s["terms"], s["weight"]

    def weight_terms(t):
        dcols = halves(d_in[t].reshape(4 * rows, part))
        weight[...] = dot3(dcols, halves(group[t].reshape(4 * rows, width)), ((0,), (0,)))
        base = t * (part // 8) * lanes

        def retile(r, carry):
            strip = weight[pl.ds(pl.multiple_of(r * 8, 8), 8)]
            for j in range(lanes):
                terms[base + r * lanes + j] = strip[:, j * 128 : (j + 1) * 128]
            return carry

        lax.fori_loop(0, part // 8, retile, 0)

    def feature_stream(t, out):
        dcols = halves(d_in[t].reshape(4 * rows, part))
        feature[t] = dot3(dcols, halves(s["w"][t]), ((1,), (0,))).reshape(4, rows, width)
        net.now += 1.0
        onward = net.copy(feature.at[t, diag], s["feature_in"].at[t, 0], to_sib)
        near = net.copy(feature.at[t, sib], s["feature_in"].at[t, 1], to_sib)
        yield near.due
        onward.wait_recv()
        s["feature_in"][t, 0] = s["feature_in"][t, 0] + feature[t, far]
        last = net.copy(s["feature_in"].at[t, 0], s["feature_sum"].at[t], to_far, ("x", 0))
        yield last.due + 8.0
        near.wait_recv()
        last.wait_recv()
        out[...] = feature[t, me] + s["feature_in"][t, 1] + s["feature_sum"][t]

    def pick(prefix, *names):
        return [s[prefix + n] for n in names]

    def stream_a(k):
        return weight_stream_a(
            net, B_TILES + k * NZ * AZ, terms, total,
            *pick("a%d" % k, "mid", "others", "every", "zl", "zr"),
        )

    def stream_b(k):
        return weight_stream_b(
            net, net.device(x=(net.x + 2) % NX), k * NY * BY, terms, total,
            *pick("b%d" % k, "mid", "own", "pair", "every", "yl", "yr", "zl", "zr"),
        )

    def in_turn(streams):
        for stream in streams:
            net.spawn(stream, next(stream))
        yield net.now

    def tower(t, out, streams):
        g, u = s["grad"][t].reshape(rows, width), unit[t]
        dz = inverse[t][:, :1] * (g - u * jnp.sum(u * g, axis=1, keepdims=True))
        for k in range(4):
            d_out[t, k] = dz[:, k * part : (k + 1) * part]
        copies = [
            net.copy(d_out.at[t, place], d_in.at[t, me], device, link)
            for place, device, link in ((far, to_far, ("x", 0)), (diag, to_diag, ("x", 0)), (sib, to_sib, None))
        ]
        d_in[t, me] = d_out[t, me]
        yield copies[1].due
        for one in copies:
            one.wait_recv()
        weight_terms(t)
        net.now += 1.0
        for several in streams:
            net.spawn(in_turn(several))
        net.spawn(feature_stream(t, out), net.now + 0.5)

    unfinished = [2, 2]

    def then(t, stream, follow):
        yield from stream
        unfinished[t] -= 1
        if unfinished[t] == 0:
            net.spawn(follow)

    image_tower = tower(0, image_out, [[stream_b(k) for k in range(B_STREAMS)]])
    text_tower = tower(
        1, text_out, [[stream_a(k) for k in range(A_STREAMS)]]
    )
    for k in range(2):
        stream = image_reduce(k)
        net.spawn(then(0, stream, image_tower), next(stream))
    image_pair = (s["image_hi"][...], s["image_lo"][...])
    grad_pair = (s["pair_hi"][...], s["pair_lo"][...])
    s["text_sum"][...] = (logit_scale * dot3(grad_pair, image_pair, ((0,), (0,)))).reshape(
        2, NY, NX, 2, 8, width
    )
    net.now += 3.0
    net.spawn(then(1, text_reduce(0, "y", "x", (NY, NX)), text_tower))
    net.spawn(then(1, text_reduce(1, "x", "y", (NX, NY)), text_tower))
    interleave(net, [])
    net.finish()


def pair_target(net, rows, core, count):
    i = lax.broadcasted_iota(jnp.int32, (count, 16 * rows), 0) + (core - net.c) * count
    i = i - net.z * rows
    j = lax.broadcasted_iota(jnp.int32, (count, 16 * rows), 1)
    half = rows // 2
    a = j - (net.y * NX + net.x) * half
    b = j - 8 * rows - (net.x * NY + net.y) * half + half
    same_a = (i == a) & (a >= 0) & (a < half)
    same_b = (i == b) & (b >= half) & (b < rows)
    return jnp.where(same_a | same_b, 1.0, 0.0)


def leave_kernel(image, text, total, image_out, text_out, first, second,
                 image_held, text_held, held, arrived, left):
    count = first.shape[0]
    third = count // 3
    moves = []
    for t, out in ((0, first), (1, second)):
        for k in range(3):
            there, here = pl.ds(t * count + k * third, third), pl.ds(k * third, third)
            moves.append((total.at[there], held.at[there], out.at[here]))
    moves += [(image, image_held, image_out), (text, text_held, text_out)]
    reads = [
        pltpu.make_async_copy(src, mid, arrived.at[k]) for k, (src, mid, _) in enumerate(moves)
    ]
    writes = [pltpu.make_async_copy(mid, out, left.at[k]) for k, (_, mid, out) in enumerate(moves)]
    for one in reads:
        one.start()
    for read, write in zip(reads, writes):
        read.wait()
        write.start()
    for one in writes:
        one.wait()


def on_device(image_features, text_features, image_proj, text_proj):
    rows, width = image_features.shape
    part = image_proj.shape[1]
    shapes = scratch_shapes(rows, width, part)
    total_shape = (2 * part // 8 * (width // 128), 8, 128)
    vmem = pl.BlockSpec(memory_space=pltpu.VMEM)
    anywhere = pl.BlockSpec(memory_space=pl.ANY)
    hbm = pl.BlockSpec(memory_space=pltpu.HBM)
    semaphores = [pltpu.SemaphoreType.DMA((n,)) for n in (COPIES, COPIES, 2)]
    grad_image, grad_text, total = pl.pallas_call(
        functools.partial(kernel, tuple(shapes)),
        out_shape=[
            jax.ShapeDtypeStruct(shape, jnp.float32)
            for shape in ((rows, width), (rows, width), total_shape)
        ],
        in_specs=[vmem, vmem, anywhere, anywhere],
        out_specs=[vmem] * 3,
        scratch_shapes=[pltpu.VMEM(shape, kind) for shape, kind in shapes.values()] + semaphores,
        compiler_params=pltpu.CompilerParams(
            collective_id=1, has_side_effects=True, vmem_limit_bytes=60 * 2**20
        ),
    )(image_features, text_features, image_proj.T, text_proj.T)
    half_shape = (part // 8 * (width // 128), 8, 128)
    grad_image, grad_text, first, second = pl.pallas_call(
        leave_kernel,
        out_shape=[
            jax.ShapeDtypeStruct(shape, jnp.float32)
            for shape in ((rows, width), (rows, width), half_shape, half_shape)
        ],
        in_specs=[hbm] * 3,
        out_specs=[hbm] * 4,
        scratch_shapes=[
            pltpu.VMEM(shape, jnp.float32) for shape in ((rows, width), (rows, width), total_shape)
        ]
        + [pltpu.SemaphoreType.DMA((8,))] * 2,
    )(grad_image, grad_text, total)

    def untiled(tiles):
        tiles = tiles.reshape(part // 8, width // 128, 8, 128).transpose(0, 2, 1, 3)
        return tiles.reshape(part, width).T

    return (grad_image, grad_text, untiled(first), untiled(second))


def solution(mesh):
    fine = Mesh(mesh.devices.reshape(NZ, NY, 2, 2, NC), ("z", "y", "xh", "xl", "core"))
    rows = P(("z", "y", "xh", "xl", "core"), None)
    cols = P(None, GROUP)
    return jax.shard_map(
        on_device,
        mesh=fine,
        in_specs=(rows, rows, cols, cols),
        out_specs=(rows, rows, cols, cols),
        check_vma=False,
    )
```
